32 devices in a mesh: req: 16 (over z, y, x), tp: 2 (over core).
Axes of the slice: x: 2, y: 2, z: 4, core: 2. Of those that a mesh axis runs over, the one named last changes fastest.
Arguments:
- tokens: bfloat16 [4096, 2048], P('req', 'tp'), may hold values from -1100 to 1100
- norm_gain: bfloat16 [2048], replicated, may hold values from 0.099609375 to 1.8984375
- norm_bias: bfloat16 [2048], replicated, may hold values from -3 to 3
- w_qkv: bfloat16 [2048, 3, 1024], P(None, None, 'tp'), may hold values from -10 to 10
- segment_ids: int32 [4096], P('req'), may hold values from 0 to 7, never falling along the last dimension, each value on 1 to 2048 neighbouring positions
- pack_lengths: int32 [1], replicated, may hold values from 3968 to 4096
- page_table: int32 [32, 2], P('req'), may hold values from 0 to 15, as said below
Outputs:
- context: bfloat16 [4096, 1024], P('req', 'tp')
- kv_cache: bfloat16 [64, 2, 128, 1024], P('req', None, None, 'tp')
The draws below stay inside these ranges and needn't reach their ends.
Inputs may be any that keep to these rules, and one draw needn't show every extreme that they name: `segment_ids`: never falling along the tokens; each id covers at most 2048 consecutive tokens and some id exactly 2048. `page_table`: row g holds the owning device and the slot of the g-th page of 128 tokens. Within each aligned group of 16 devices, the j-th page of every device goes the same number of devices forward, 1 to 8, into slot j, unless that passes the last device of the axis; then it stays on its own device in slot j + 2.
All inputs are finite; a program needn't handle non-finite values.
Results may differ from the reference program's by a relative error of at most 0.0099.
Values may be sent and summed in bfloat16 or wider, within the bound.
No kernel may reach another device: no remote copies, remote signals or barrier semaphores. Data moves between devices by JAX's collectives and lax.ppermute only.
A program may use at most 64 MiB of HBM per device.

```python
import math
import jax
import jax.numpy as jnp
import numpy as np
from jax import lax

D = 2048
HEADS = 8
HD = 128
PAGE = 128
SEG_MAX = 2048
TOK_DEV = 256
HH = 1024
TOKENS = 4096
PACK_LEN = 4096
PACKS = 1
REACH = 8
SLOTS = 4
NPAGES = 32
N_REQ = 16


def draw_tokens(key, part):
    drawn_base = jax.random.truncated_normal(jax.random.fold_in(key, 1), -6.0, 6.0, (TOKENS, D), jnp.float32)
    column_scale = jnp.exp(jax.random.uniform(jax.random.fold_in(key, 3), (1, D), jnp.float32) * math.log(10.0))
    row_scale = jnp.exp(jax.random.uniform(jax.random.fold_in(key, 2), (TOKENS, 1), jnp.float32) * math.log(10.0))
    return (drawn_base * row_scale * column_scale).astype(jnp.bfloat16)


def draw_w_qkv(key, part):
    factor = D ** (-0.5)
    query_side = jax.random.truncated_normal(jax.random.fold_in(key, 1), -6.0, 6.0, (D, HH), jnp.float32) * factor
    key_side = jax.random.truncated_normal(jax.random.fold_in(key, 3), -6.0, 6.0, (D, HH), jnp.float32) * factor
    value_side = jax.random.truncated_normal(jax.random.fold_in(key, 4), -6.0, 6.0, (D, HH), jnp.float32) * factor
    return jnp.stack([query_side, key_side, value_side], axis=1).astype(jnp.bfloat16)


def draw_page_table(key, part):
    per_pack = PACK_LEN // TOK_DEV
    pages_dev = TOK_DEV // PAGE
    device_count = TOKENS // TOK_DEV
    forward = jax.random.randint(jax.random.fold_in(key, 11), (PACKS, pages_dev), 1, REACH + 1, jnp.int32)
    page_ids = jnp.arange(NPAGES, dtype=jnp.int32)
    device = page_ids // pages_dev
    column = page_ids % pages_dev
    pack_ids = device // per_pack
    forward_by = forward[pack_ids, column]
    goes_ahead = device + forward_by <= device_count - 1
    owner_ids = jnp.where(goes_ahead, device + forward_by, device)
    slot_ids = jnp.where(goes_ahead, column, column + pages_dev)
    return jnp.stack([owner_ids, slot_ids], axis=1).astype(jnp.int32)


def profile(amount, total, limit, skew):
    portions = [(1 << 20) // math.isqrt(rank ** skew) + 1 for rank in range(2, amount + 1)]
    rest, counts = total - limit - (amount - 1), [1] * (amount - 1)
    while rest > 0:
        free = [i for i in range(amount - 1) if counts[i] < limit]
        mass, left = sum([portions[i] for i in free]), rest
        for i in free:
            more = min(limit - counts[i], max(1, left * portions[i] // mass), rest)
            counts[i] = counts[i] + more
            rest = rest - more
    return np.array([limit] + counts)


def uneven(key, number_of, total, bound, skew):
    if number_of == 2:
        one = jax.random.randint(key, (), max(1, total - bound), min(bound, total - 1) + 1)
        return jnp.stack([one, total - one])
    tallies = jnp.asarray(profile(number_of, total, bound, skew), jnp.int32)
    pairs = (number_of - 1) // 2
    giver, receiver = tallies[1:1 + 2 * pairs:2], tallies[2:2 + 2 * pairs:2]
    slack = jnp.minimum(giver - 1, bound - receiver)
    moved = jax.random.randint(jax.random.fold_in(key, 1), (pairs,), 0, 1 << 20) % (slack + 1)
    tallies = tallies.at[1:1 + 2 * pairs:2].set(giver - moved).at[2:2 + 2 * pairs:2].set(receiver + moved)
    return tallies[jax.random.permutation(jax.random.fold_in(key, 2), number_of)]


def scatter_about(stream_key, extent, spread, limit, kind=jnp.bfloat16):
    entries = spread * jax.random.normal(stream_key, extent, jnp.float32)
    return jnp.clip(entries, min=-limit, max=limit).astype(kind)


def setup_inputs(seed: int = 0) -> dict:
    arg_keys = jax.random.split(jax.random.key(seed), 8)
    return {
        "tokens": draw_tokens(jax.random.fold_in(arg_keys[7], 71), 0),
        "norm_gain": jnp.clip(1.0 + 0.18 * jax.random.normal(arg_keys[1], (D,), jnp.float32), 0.099609375, 1.8984375).astype(jnp.bfloat16),
        "norm_bias": scatter_about(arg_keys[2], (D,), 0.5, 3.0),
        "w_qkv": draw_w_qkv(jax.random.fold_in(arg_keys[7], 71), 0),
        "segment_ids": jnp.searchsorted(jnp.cumsum(uneven(arg_keys[4], TOKENS // SEG_MAX * 4, TOKENS, SEG_MAX, 2)), jnp.arange(TOKENS), side="right").astype(jnp.int32),
        "pack_lengths": jax.random.randint(arg_keys[5], (PACKS,), PACK_LEN - TOK_DEV // 2, PACK_LEN + 1).astype(jnp.int32),
        "page_table": draw_page_table(jax.random.fold_in(arg_keys[7], 71), 0),
    }


def layer_norm(features, norm_gain, norm_bias):
    as_float = features.astype(jnp.float32)
    row_mean = lax.optimization_barrier(jnp.mean(as_float, axis=-1, keepdims=True))
    centred = as_float - row_mean
    variance = lax.optimization_barrier(jnp.mean(centred * centred, axis=-1, keepdims=True))
    scaled = centred * lax.rsqrt(variance + 1e-05)
    return (scaled * norm_gain.astype(jnp.float32) + norm_bias.astype(jnp.float32)).astype(jnp.bfloat16)

def reference(tokens, norm_gain, norm_bias, w_qkv, segment_ids, pack_lengths, page_table):
    normed = layer_norm(tokens, norm_gain, norm_bias)
    projected = jnp.dot(normed, w_qkv.reshape(D, 3 * HH), preferred_element_type=jnp.float32).reshape(TOKENS, 3, HH)
    positions = jnp.arange(TOKENS, dtype=jnp.int32)
    in_length = (positions % PACK_LEN < pack_lengths[positions // PACK_LEN])[:, None]
    queries = (projected[:, 0] * HD ** (-0.5)).astype(jnp.bfloat16)
    key_rows = jnp.where(in_length, projected[:, 1], 0.0).astype(jnp.bfloat16)
    value_rows = jnp.where(in_length, projected[:, 2], 0.0).astype(jnp.bfloat16)
    window = REACH * TOK_DEV
    padded_keys = jnp.concatenate([jnp.zeros((window, HH), jnp.bfloat16), key_rows], axis=0)
    padded_values = jnp.concatenate([jnp.zeros((window, HH), jnp.bfloat16), value_rows], axis=0)
    padded_ids = jnp.concatenate([jnp.full((window,), -1, jnp.int32), segment_ids.astype(jnp.int32)], axis=0)

    def attend_block(block_index):
        first = (block_index * TOK_DEV).astype(jnp.int32)
        query_part = lax.dynamic_slice_in_dim(queries, first, TOK_DEV, 0)
        query_ids = lax.dynamic_slice_in_dim(segment_ids.astype(jnp.int32), first, TOK_DEV, 0)
        key_part = lax.dynamic_slice_in_dim(padded_keys, first, window + TOK_DEV, 0)
        value_part = lax.dynamic_slice_in_dim(padded_values, first, window + TOK_DEV, 0)
        key_ids = lax.dynamic_slice_in_dim(padded_ids, first, window + TOK_DEV, 0)
        query_pos = first + jnp.arange(TOK_DEV, dtype=jnp.int32)
        key_pos = first - window + jnp.arange(window + TOK_DEV, dtype=jnp.int32)
        allowed = (key_pos >= 0)[None, :] & (key_pos[None, :] <= query_pos[:, None])
        allowed = allowed & (key_ids[None, :] == query_ids[:, None])
        allowed = allowed & ((key_pos // PACK_LEN)[None, :] == (query_pos // PACK_LEN)[:, None])
        query_heads = query_part.astype(jnp.float32).reshape(TOK_DEV, HEADS, HD)
        key_heads = key_part.astype(jnp.float32).reshape(window + TOK_DEV, HEADS, HD)
        value_heads = value_part.astype(jnp.float32).reshape(window + TOK_DEV, HEADS, HD)
        scores = jnp.einsum('qhd,khd->hqk', query_heads, key_heads)
        scores = jnp.where(allowed[None], scores, -1e+30)
        row_max = lax.optimization_barrier(jnp.max(scores, axis=2, keepdims=True))
        exp_scores = jnp.exp(scores - row_max)
        row_sum = lax.optimization_barrier(jnp.sum(exp_scores, axis=2, keepdims=True))
        probs_bf = (exp_scores / row_sum).astype(jnp.bfloat16)
        mixed = jnp.einsum('hqk,khd->qhd', probs_bf.astype(jnp.float32), value_heads)
        return mixed.reshape(TOK_DEV, HH)
    context_all = lax.map(attend_block, jnp.arange(TOKENS // TOK_DEV, dtype=jnp.int32)).reshape(TOKENS, HH)
    context = jnp.where(in_length, context_all, 0.0).astype(jnp.bfloat16)
    page_data = jnp.stack([key_rows.reshape(NPAGES, PAGE, HH), value_rows.reshape(NPAGES, PAGE, HH)], axis=1)
    target = (page_table[:, 0] * SLOTS + page_table[:, 1]).astype(jnp.int32)
    kv_cache = jnp.zeros((N_REQ * SLOTS, 2, PAGE, HH), jnp.bfloat16).at[target].set(page_data)
    return (context, kv_cache)
```

```python
import functools
import jax
import jax.numpy as jnp
from jax import lax
from jax.experimental import pallas as pl
from jax.experimental.pallas import tpu as pltpu
from jax.sharding import PartitionSpec as P

HD = 128
PAGE = 128
REACH = 8
NOTES = 16
MASKED = -1e30
VMEM = pl.BlockSpec(memory_space=pltpu.VMEM)
SMEM = pl.BlockSpec(memory_space=pltpu.SMEM)


def paired(shard, axis, bit):
    devices = lax.axis_size(axis)
    return lax.ppermute(shard, axis, [(i, i ^ bit) for i in range(devices)])


def forward(shard, axis, by):
    devices = lax.axis_size(axis)
    return lax.ppermute(shard, axis, [(i, i + by) for i in range(devices - by)])


def cost(flops, moved, transcendentals=0):
    return pl.CostEstimate(flops=flops, bytes_accessed=moved, transcendentals=transcendentals)


def valid_rows(lengths_ref, row_count):
    device = lax.axis_index("req")
    per_pack = lax.axis_size("req") // lengths_ref.shape[0]
    limit = lengths_ref[device // per_pack] - device % per_pack * row_count
    return lax.broadcasted_iota(jnp.int32, (row_count, 1), 0) < limit


def key_value_kernel(tp, heads, lengths_ref, table_ref, notes_ref, *refs):
    parts, refs = refs[:tp], refs[tp:]
    gain_ref, bias_ref, w_ref, normed_ref = refs[:4]
    sends, (columns,) = refs[4 : 4 + 2 * heads], refs[4 + 2 * heads :]
    rows, features = parts[0].shape
    here = lax.axis_index("tp")
    me = lax.axis_index("req") % heads
    which = pl.program_id(0)

    @pl.when(which == 0)
    def _():
        step = 32

        def norm_rows(index, carry):
            at = pl.ds(pl.multiple_of(index * step, step), step)
            pieces = [part[at, :].astype(jnp.float32) for part in parts]
            total = sum(jnp.sum(piece, axis=1, keepdims=True) for piece in pieces)
            mean = total * (1.0 / (tp * features))
            centred = [piece - mean for piece in pieces]
            squares = sum(jnp.sum(piece * piece, axis=1, keepdims=True) for piece in centred)
            scale = lax.rsqrt(squares * (1.0 / (tp * features)) + 1e-05)
            for bit, piece in enumerate(centred):
                lanes = pl.ds(pl.multiple_of((here ^ bit) * features, features), features)
                gain = gain_ref[:, lanes].astype(jnp.float32)
                bias = bias_ref[:, lanes].astype(jnp.float32)
                normed_ref[at, lanes] = (piece * scale * gain + bias).astype(jnp.bfloat16)
            return carry

        lax.fori_loop(0, rows // step, norm_rows, 0)

    projected = jnp.dot(normed_ref[...], w_ref[0], preferred_element_type=jnp.float32)
    projected = jnp.where(valid_rows(lengths_ref, rows), projected, 0.0)
    columns[...] = projected.astype(jnp.bfloat16)
    for bit in range(heads):
        lanes = pl.ds(pl.multiple_of((me ^ bit) * HD, HD), HD)
        for page in range(2):
            at = pl.ds(pl.multiple_of(which * PAGE, PAGE), PAGE)
            sends[2 * bit + page][at, :] = columns[page * PAGE : (page + 1) * PAGE, lanes]

    @pl.when(which == 1)
    def _():
        row = lax.broadcasted_iota(jnp.int32, (NOTES, HD), 0)
        notes = jnp.zeros((NOTES, HD), jnp.int32)
        for page in range(2):
            notes = jnp.where(row == page, notes_ref[:, page * PAGE : (page + 1) * PAGE] + 1, notes)
            for column in range(2):
                entry = table_ref[page, column] + 1
                notes = jnp.where(row == 2 + 2 * page + column, entry, notes)
        notes = notes.astype(jnp.float32).astype(jnp.bfloat16)
        for bit in range(heads):
            sends[2 * bit][2 * PAGE :, :] = notes


def query_kernel(heads, normed_ref, w_ref, *refs):
    sends, columns = refs[:heads], refs[heads]
    me = lax.axis_index("req") % heads
    projected = jnp.dot(normed_ref[...], w_ref[0], preferred_element_type=jnp.float32)
    columns[...] = (projected * HD ** (-0.5)).astype(jnp.bfloat16)
    for bit in range(heads):
        sends[bit][...] = columns[:, pl.ds(pl.multiple_of((me ^ bit) * HD, HD), HD)]


def attend_kernel(heads, reach, packs, tiles, first, last, cache_page, *refs):
    refs = list(refs)
    take = lambda count: [refs.pop(0) for _ in range(count)]
    queries = take(heads)
    noted = dict(zip(noted_layers(reach, tiles, cache_page), take(len(noted_layers(reach, tiles, cache_page)))))
    pages = dict(zip(page_list(reach, tiles, cache_page), take(len(page_list(reach, tiles, cache_page)))))
    pages.update({(layer, 0): buffer for layer, buffer in noted.items()})
    state = [] if first else take(2)
    outs = refs
    device = lax.axis_index("req")
    per_pack = lax.axis_size("req") // packs
    me = device % heads
    rows = queries[0].shape[0]
    width = heads * PAGE
    notes = {
        layer: [buffer[bit, 2 * PAGE :, :].astype(jnp.float32) for bit in range(heads)]
        for layer, buffer in noted.items()
    }
    keys, values, key_ids, key_places = [], [], [], []
    ones = jnp.ones((width, HD), jnp.bfloat16)
    lane = lax.broadcasted_iota(jnp.int32, (1, PAGE), 1)
    for layer, page in tiles:
        buffer = pages[layer, page]
        keys.append(buffer[:, :PAGE].reshape(width, HD))
        values.append(
            jnp.concatenate([buffer[:, PAGE : 2 * PAGE].reshape(width, HD), ones], axis=1)
        )
        ids = jnp.concatenate([note[page : page + 1] for note in notes[layer]], axis=1)
        if layer > 0:
            same_pack = (device - layer * heads) // per_pack == device // per_pack
            ids = jnp.where(same_pack, ids, 0.0)
        key_ids.append(ids)
        key_places.append(
            jnp.concatenate(
                [lane + ((me ^ bit) * rows + page * PAGE) for bit in range(heads)], axis=1
            )
        )
    for bit in range(heads):
        query = queries[bit][...]
        query_ids = jnp.concatenate(
            [
                jnp.broadcast_to(notes[0][bit][page : page + 1], (PAGE, PAGE)).T[:, :1]
                for page in range(2)
            ],
            axis=0,
        )
        place = lax.broadcasted_iota(jnp.int32, (rows, 1), 0) + (me ^ bit) * rows
        if first:
            top = jnp.full((rows, 1), MASKED, jnp.float32)
            total = jnp.zeros((rows, 2 * HD), jnp.float32)
        else:
            top = state[0][bit][:, :1]
            total = state[1][bit]
        for index, (layer, page) in enumerate(tiles):
            scores = lax.dot_general(
                query, keys[index], (((1,), (1,)), ((), ())), preferred_element_type=jnp.float32
            )
            allowed = key_ids[index] == query_ids
            if layer == 0:
                allowed = allowed & (key_places[index] <= place)
            scores = jnp.where(allowed, scores, MASKED)
            higher = jnp.maximum(top, jnp.max(scores, axis=1, keepdims=True))
            weights = jnp.exp(scores - higher).astype(jnp.bfloat16)
            total = total * jnp.exp(top - higher) + jnp.dot(
                weights, values[index], preferred_element_type=jnp.float32
            )
            top = higher
        if last:
            outs[bit][0:rows, :] = (total[:, :HD] / total[:, HD:]).astype(jnp.bfloat16)
        else:
            outs[0][bit] = jnp.broadcast_to(top, (rows, HD))
            outs[1][bit] = total
    if cache_page is not None:
        start = rows if last else 0
        outs = outs if last else outs[2:]
        for bit in range(heads):
            owner = (device ^ bit) + 1
            found = jnp.zeros((2 * PAGE, HD), jnp.bfloat16)
            for layer in range(reach + 1):
                for other in range(heads):
                    if layer == 0 and other == bit:
                        continue
                    note = notes[layer][other]
                    at = 2 + 2 * cache_page
                    hit = (note[at : at + 1] == owner.astype(jnp.float32)) & (
                        note[at + 1 : at + 2] == cache_page + 1.0
                    )
                    page = pages[layer, cache_page][other, : 2 * PAGE, :]
                    found = jnp.where(hit, page, found)
            outs[bit][start : start + 2 * PAGE, :] = found


def noted_layers(reach, tiles, cache_page):
    layers = range(reach + 1) if cache_page is not None else [0] + [layer for layer, _ in tiles]
    return sorted(set(layers))


def page_list(reach, tiles, cache_page):
    wanted = list(tiles)
    if cache_page is not None:
        wanted += [(layer, cache_page) for layer in range(reach + 1)]
    return sorted(set(place for place in wanted if place[1] == 1))


def finish_kernel(heads, table_ref, lengths_ref, *refs):
    refs = list(refs)
    take = lambda count: [refs.pop(0) for _ in range(count)]
    final, early, own = take(heads), take(heads), take(2 * heads)
    context_ref, cache_ref = refs
    device = lax.axis_index("req")
    me = device % heads
    rows = context_ref.shape[0]
    valid = valid_rows(lengths_ref, rows)
    for bit in range(heads):
        lanes = pl.ds(pl.multiple_of((me ^ bit) * HD, HD), HD)
        context_ref[:, lanes] = jnp.where(valid, final[bit][0:rows, :], 0).astype(jnp.bfloat16)
        for part in range(2):
            first = part * PAGE
            cache_ref[0, part, :, lanes] = early[bit][first : first + PAGE, :]
            cache_ref[1, part, :, lanes] = final[bit][rows + first : rows + first + PAGE, :]
            for page in range(2):
                stays = (table_ref[page, 0] == device) & (table_ref[page, 1] == page + 2)
                cache_ref[2 + page, part, :, lanes] = jnp.where(
                    stays, own[2 * bit + page][first : first + PAGE, :], 0
                ).astype(jnp.bfloat16)


def per_device(tokens, norm_gain, norm_bias, w_qkv, segment_ids, pack_lengths, page_table):
    rows, features = tokens.shape
    tp = lax.axis_size("tp")
    local_width = w_qkv.shape[2]
    heads = local_width // HD
    reach = REACH // heads
    width = w_qkv.shape[0]
    packs = pack_lengths.shape[0]
    bf16 = jnp.bfloat16

    parts = [tokens] + [paired(tokens, "tp", bit) for bit in range(1, tp)]
    weights = jnp.transpose(w_qkv, (1, 0, 2))
    gain, bias = norm_gain.reshape(1, -1), norm_bias.reshape(1, -1)

    page_shapes = [(2 * PAGE + NOTES, HD), (2 * PAGE, HD)] * heads
    whole = lambda shape: pl.BlockSpec(shape, lambda i: (0,) * len(shape))
    normed, *own = pl.pallas_call(
        functools.partial(key_value_kernel, tp, heads),
        grid=(2,),
        out_shape=[jax.ShapeDtypeStruct((rows, width), bf16)] + [jax.ShapeDtypeStruct(shape, bf16) for shape in page_shapes],
        in_specs=[SMEM, SMEM, whole((1, rows))]
        + [whole((rows, features))] * tp
        + [whole((1, width))] * 2
        + [pl.BlockSpec((1, width, local_width), lambda i: (i + 1, 0, 0))],
        out_specs=[whole((rows, width))] + [whole(shape) for shape in page_shapes],
        scratch_shapes=[pltpu.VMEM((rows, local_width), bf16)],
        compiler_params=pltpu.CompilerParams(vmem_limit_bytes=24 << 20),
        cost_estimate=cost(4 * rows * width * local_width, 4 * width * local_width),
        name="norm_keys_values",
    )(pack_lengths, page_table, segment_ids.reshape(1, rows), *parts, gain, bias, weights)

    received = [
        [own[page]] + [paired(own[2 * bit + page], "req", bit) for bit in range(1, heads)]
        for page in range(2)
    ]
    layers = [[jnp.stack(pieces) for pieces in received]]

    queries = pl.pallas_call(
        functools.partial(query_kernel, heads),
        grid=(1,),
        out_shape=[jax.ShapeDtypeStruct((rows, HD), bf16)] * heads,
        in_specs=[
            whole((rows, width)),
            pl.BlockSpec((1, width, local_width), lambda i: (0, 0, 0)),
        ],
        out_specs=[whole((rows, HD))] * heads,
        scratch_shapes=[pltpu.VMEM((rows, local_width), bf16)],
        compiler_params=pltpu.CompilerParams(vmem_limit_bytes=24 << 20),
        cost_estimate=cost(2 * rows * width * local_width, 2 * width * local_width),
        name="queries",
    )(normed, weights)
    queries = [queries[0]] + [paired(queries[bit], "req", bit) for bit in range(1, heads)]

    for _ in range(reach):
        layers.append([forward(buffer, "req", heads) for buffer in layers[-1]])

    state_shape = [
        jax.ShapeDtypeStruct((heads, rows, HD), jnp.float32),
        jax.ShapeDtypeStruct((heads, rows, 2 * HD), jnp.float32),
    ]

    def attend(tiles, state, last, cache_page):
        pairs = heads * rows * heads * PAGE * len(tiles)
        operands = (
            list(queries)
            + [layers[layer][0] for layer in noted_layers(reach, tiles, cache_page)]
            + [layers[layer][page] for layer, page in page_list(reach, tiles, cache_page)]
            + list(state)
        )
        if last:
            outs = [jax.ShapeDtypeStruct((rows + 2 * PAGE, HD), bf16)] * heads
        else:
            outs = state_shape + (
                [jax.ShapeDtypeStruct((2 * PAGE, HD), bf16)] * heads
                if cache_page is not None
                else []
            )
        return pl.pallas_call(
            functools.partial(
                attend_kernel, heads, reach, packs, tiles, not state, last, cache_page
            ),
            out_shape=outs,
            in_specs=[VMEM] * len(operands),
            out_specs=[VMEM] * len(outs),
            compiler_params=pltpu.CompilerParams(vmem_limit_bytes=32 << 20),
            cost_estimate=cost(6 * pairs * HD, 4 << 20, pairs),
            name="attend",
        )(*operands)

    state = attend([(0, 0), (0, 1)], [], False, None)
    for layer in range(1, reach):
        state = attend([(layer, 0), (layer, 1)], state, False, None)
    *state, = attend([(reach, 0)], state, False, 0)
    state, early = state[:2], state[2:]
    early = [early[0]] + [paired(early[bit], "req", bit) for bit in range(1, heads)]
    final = attend([(reach, 1)], state, True, 1)
    final = [final[0]] + [paired(final[bit], "req", bit) for bit in range(1, heads)]

    context, cache = pl.pallas_call(
        functools.partial(finish_kernel, heads),
        out_shape=[
            jax.ShapeDtypeStruct((rows, local_width), bf16),
            jax.ShapeDtypeStruct((4, 2, PAGE, local_width), bf16),
        ],
        in_specs=[SMEM, SMEM] + [VMEM] * (4 * heads),
        out_specs=[VMEM] * 2,
        compiler_params=pltpu.CompilerParams(vmem_limit_bytes=16 << 20),
        name="finish",
    )(page_table, pack_lengths, *final, *early, *own)
    return context, cache


def solution(mesh):
    return jax.shard_map(
        per_device,
        mesh=mesh,
        in_specs=(P("req", "tp"), P(), P(), P(None, None, "tp"), P("req"), P(), P("req", None)),
        out_specs=(P("req", "tp"), P("req", None, None, "tp")),
        check_vma=False,
    )
```

```python
import functools
import jax
import jax.numpy as jnp
from jax import lax
from jax.experimental import pallas as pl
from jax.experimental.pallas import tpu as pltpu
from jax.sharding import PartitionSpec as P

HD = 128
PAGE = 128
REACH = 8
NOTES = 16
MASKED = -1e30
PROJECT_VMEM = 48 << 20
VMEM = pl.BlockSpec(memory_space=pltpu.VMEM)
SMEM = pl.BlockSpec(memory_space=pltpu.SMEM)
HBM = pl.BlockSpec(memory_space=pltpu.HBM)


def paired(shard, axis, bit):
    devices = lax.axis_size(axis)
    return lax.ppermute(shard, axis, [(i, i ^ bit) for i in range(devices)])


def forward(shard, axis, by):
    devices = lax.axis_size(axis)
    return lax.ppermute(shard, axis, [(i, i + by) for i in range(devices - by)])


def cost(flops, moved, transcendentals=0):
    return pl.CostEstimate(flops=flops, bytes_accessed=moved, transcendentals=transcendentals)


def valid_rows(lengths_ref, row_count):
    device = lax.axis_index("req")
    per_pack = lax.axis_size("req") // lengths_ref.shape[0]
    limit = lengths_ref[device // per_pack] - device % per_pack * row_count
    return lax.broadcasted_iota(jnp.int32, (row_count, 1), 0) < limit


def project_kernel(tp, heads, *refs):
    refs = list(refs)
    take = lambda count: [refs.pop(0) for _ in range(count)]
    lengths_ref, tokens_hbm, w_hbm, affine_ref, notes_ref = take(5)
    received, (normed_ref,), pieces = take(tp - 1), take(1), take(2 * heads)
    tokens_ref, w_ref, spread_ref, columns, sems = refs
    rows, features = tokens_ref.shape
    here = lax.axis_index("tp")
    me = lax.axis_index("req") % heads
    loads = [
        pltpu.make_async_copy(tokens_hbm, tokens_ref, sems.at[0]),
        pltpu.make_async_copy(w_hbm.at[1], w_ref.at[0], sems.at[1]),
        pltpu.make_async_copy(w_hbm.at[2], w_ref.at[1], sems.at[2]),
    ]
    for load in loads:
        load.start()
    lines = affine_ref.shape[0] // 2
    affine = affine_ref[...].astype(jnp.float32)
    for row in range(2):
        for line in range(lines):
            spread_ref[row : row + 1, line * HD : (line + 1) * HD] = affine[
                row * lines + line : row * lines + line + 1
            ]
    loads[0].wait()
    parts = [tokens_ref] + received
    step = 32

    def norm_rows(index, carry):
        at = pl.ds(pl.multiple_of(index * step, step), step)
        shares = [part[at, :].astype(jnp.float32) for part in parts]
        total = sum(jnp.sum(share, axis=1, keepdims=True) for share in shares)
        mean = total * (1.0 / (tp * features))
        centred = [share - mean for share in shares]
        squares = sum(jnp.sum(share * share, axis=1, keepdims=True) for share in centred)
        scale = lax.rsqrt(squares * (1.0 / (tp * features)) + 1e-05)
        for bit, share in enumerate(centred):
            lanes = pl.ds(pl.multiple_of((here ^ bit) * features, features), features)
            gain = spread_ref[0:1, lanes]
            bias = spread_ref[1:2, lanes]
            normed_ref[at, lanes] = (share * scale * gain + bias).astype(jnp.bfloat16)
        return carry

    lax.fori_loop(0, rows // step, norm_rows, 0)

    valid = valid_rows(lengths_ref, rows)
    for which in range(2):
        loads[1 + which].wait()
        projected = jnp.dot(normed_ref[...], w_ref[which], preferred_element_type=jnp.float32)
        columns[...] = jnp.where(valid, projected, 0.0).astype(jnp.bfloat16)
        for bit in range(heads):
            lanes = pl.ds(pl.multiple_of((me ^ bit) * HD, HD), HD)
            for page in range(2):
                pieces[2 * bit + page][which * PAGE : (which + 1) * PAGE, :] = columns[
                    page * PAGE : (page + 1) * PAGE, lanes
                ]

    for bit in range(heads):
        pieces[2 * bit][2 * PAGE :, :] = notes_ref[...]


def query_kernel(heads, normed_ref, w_hbm, *refs):
    pieces, (columns, w_ref, sem) = refs[:heads], refs[heads:]
    load = pltpu.make_async_copy(w_hbm.at[0], w_ref, sem)
    load.start()
    load.wait()
    me = lax.axis_index("req") % heads
    projected = jnp.dot(normed_ref[...], w_ref[...], preferred_element_type=jnp.float32)
    columns[...] = (projected * HD ** (-0.5)).astype(jnp.bfloat16)
    for bit in range(heads):
        pieces[bit][...] = columns[:, pl.ds(pl.multiple_of((me ^ bit) * HD, HD), HD)]


def attend_kernel(heads, reach, packs, tiles, first, last, cache_page, *refs):
    refs = list(refs)
    take = lambda count: [refs.pop(0) for _ in range(count)]
    queries = take(heads)
    noted = dict(zip(noted_layers(reach, tiles, cache_page), take(len(noted_layers(reach, tiles, cache_page)))))
    pages = dict(zip(page_list(reach, tiles, cache_page), take(len(page_list(reach, tiles, cache_page)))))
    pages.update({(layer, 0): buffer for layer, buffer in noted.items()})
    ids_ref, top_ref, total_ref = (None,) * 3 if first else take(3)
    if first:
        ids_ref = take(1)[0]
    top_out, total_out = (None,) * 2 if last else take(2)
    outs = refs
    device = lax.axis_index("req")
    per_pack = lax.axis_size("req") // packs
    me = device % heads
    rows = 2 * PAGE
    width = heads * PAGE
    notes = {
        layer: [buffer[bit, 2 * PAGE :, :].astype(jnp.float32) for bit in range(heads)]
        for layer, buffer in noted.items()
    }
    keys, values, key_ids, key_places = [], [], [], []
    ones = jnp.ones((width, HD), jnp.bfloat16)
    lane = lax.broadcasted_iota(jnp.int32, (1, PAGE), 1)
    for layer, page in tiles:
        buffer = pages[layer, page]
        keys.append(buffer[:, :PAGE].reshape(width, HD))
        values.append(
            jnp.concatenate([buffer[:, PAGE : 2 * PAGE].reshape(width, HD), ones], axis=1)
        )
        ids = jnp.concatenate([note[page : page + 1] for note in notes[layer]], axis=1)
        if layer > 0:
            same_pack = (device - layer * heads) // per_pack == device // per_pack
            ids = jnp.where(same_pack, ids, 0.0)
        key_ids.append(ids)
        key_places.append(
            jnp.concatenate(
                [lane + ((me ^ bit) * rows + page * PAGE) for bit in range(heads)], axis=1
            )
        )
    wide = (PAGE, HD)
    for bit in range(heads):
        for page in range(2):
            at = pl.ds(page * PAGE, PAGE)
            query = queries[bit][at, :]
            if first:
                query_ids = jnp.broadcast_to(notes[0][bit][page : page + 1], wide).T
                ids_ref[bit, at] = query_ids
                place = lax.broadcasted_iota(jnp.int32, wide, 0) + ((me ^ bit) * rows + page * PAGE)
                top = jnp.full(wide, MASKED, jnp.float32)
                total = [jnp.zeros(wide, jnp.float32)] * 2
            else:
                query_ids = ids_ref[bit, at]
                top = top_ref[bit, at]
                total = [total_ref[bit, at, half * HD : (half + 1) * HD] for half in range(2)]
            for index, (layer, _) in enumerate(tiles):
                scores = lax.dot_general(
                    query, keys[index], (((1,), (1,)), ((), ())), preferred_element_type=jnp.float32
                )
                chunks = []
                for other in range(heads):
                    lanes = slice(other * PAGE, (other + 1) * PAGE)
                    allowed = key_ids[index][:, lanes] == query_ids
                    if layer == 0:
                        allowed = allowed & (key_places[index][:, lanes] <= place)
                    chunks.append(jnp.where(allowed, scores[:, lanes], MASKED))
                highest = jnp.max(functools.reduce(jnp.maximum, chunks), axis=1, keepdims=True)
                higher = jnp.maximum(top, jnp.broadcast_to(highest, wide))
                weights = jnp.concatenate(
                    [jnp.exp(chunk - higher).astype(jnp.bfloat16) for chunk in chunks], axis=1
                )
                shrink = jnp.exp(top - higher)
                added = jnp.dot(weights, values[index], preferred_element_type=jnp.float32)
                total = [total[half] * shrink + added[:, half * HD : (half + 1) * HD] for half in range(2)]
                top = higher
            if last:
                outs[bit][at, :] = (total[0] / total[1]).astype(jnp.bfloat16)
            else:
                top_out[bit, at] = top
                for half in range(2):
                    total_out[bit, at, half * HD : (half + 1) * HD] = total[half]
    if cache_page is not None:
        select_pages(heads, reach, cache_page, device, notes, pages, outs, rows)


def select_pages(heads, reach, page, device, notes, pages, outs, start):
    me = device % heads
    sought = jnp.zeros((1, HD), jnp.int32)
    for bit in range(heads):
        owner = ((device ^ bit) + 1).astype(jnp.float32)
        for layer in range(reach + 1):
            for other in range(heads):
                if layer == 0 and other == bit:
                    continue
                note = notes[layer][other]
                at = 2 + 2 * page
                hit = (note[at : at + 1] == owner) & (note[at + 1 : at + 2] == page + 1.0)
                place = (layer * heads + other + 1) << (6 * bit)
                sought = sought | jnp.where(hit, place, 0)
    sought = jnp.max(sought)
    for bit in range(heads):
        found = ((sought >> (6 * bit)) & 63) - 1
        for layer in range(reach + 1):

            @pl.when((found >= layer * heads) & (found < (layer + 1) * heads))
            def _():
                outs[bit][start : start + 2 * PAGE, :] = pages[layer, page][
                    found - layer * heads, : 2 * PAGE, :
                ]

        @pl.when(found < 0)
        def _():
            outs[bit][start : start + 2 * PAGE, :] = jnp.zeros((2 * PAGE, HD), jnp.bfloat16)


def select_kernel(heads, reach, *refs):
    buffers, outs = refs[: reach + 1], refs[reach + 1 :]
    notes = [
        [buffer[bit, 2 * PAGE :, :].astype(jnp.float32) for bit in range(heads)]
        for buffer in buffers
    ]
    pages = {(layer, 0): buffer for layer, buffer in enumerate(buffers)}
    select_pages(heads, reach, 0, lax.axis_index("req"), notes, pages, outs, 0)


def noted_layers(reach, tiles, cache_page):
    layers = range(reach + 1) if cache_page is not None else [0] + [layer for layer, _ in tiles]
    return sorted(set(layers))


def page_list(reach, tiles, cache_page):
    wanted = list(tiles)
    if cache_page is not None:
        wanted += [(layer, cache_page) for layer in range(reach + 1)]
    return sorted(set(place for place in wanted if place[1] == 1))


def finish_kernel(heads, table_hbm, lengths_ref, *refs):
    refs = list(refs)
    take = lambda count: [refs.pop(0) for _ in range(count)]
    final, early, own = take(heads), take(heads), take(2 * heads)
    context_ref, cache_ref, table_ref, sem = refs
    load = pltpu.make_async_copy(table_hbm, table_ref, sem)
    load.start()
    load.wait()
    device = lax.axis_index("req")
    me = device % heads
    rows = context_ref.shape[0]
    valid = valid_rows(lengths_ref, rows)
    for bit in range(heads):
        lanes = pl.ds(pl.multiple_of((me ^ bit) * HD, HD), HD)
        context_ref[:, lanes] = jnp.where(valid, final[bit][0:rows, :], 0).astype(jnp.bfloat16)
        for part in range(2):
            first = part * PAGE
            cache_ref[0, part, :, lanes] = early[bit][first : first + PAGE, :]
            cache_ref[1, part, :, lanes] = final[bit][rows + first : rows + first + PAGE, :]
            for page in range(2):
                stays = (table_ref[page, 0] == device) & (table_ref[page, 1] == page + 2)
                cache_ref[2 + page, part, :, lanes] = jnp.where(
                    stays, own[2 * bit + page][first : first + PAGE, :], 0
                ).astype(jnp.bfloat16)


def per_device(tokens, norm_gain, norm_bias, w_qkv, segment_ids, pack_lengths, page_table):
    rows, features = tokens.shape
    tp = lax.axis_size("tp")
    local_width = w_qkv.shape[2]
    heads = local_width // HD
    reach = REACH // heads
    width = w_qkv.shape[0]
    packs = pack_lengths.shape[0]
    bf16 = jnp.bfloat16

    received = [paired(tokens, "tp", bit) for bit in range(1, tp)]
    weights = jnp.transpose(w_qkv, (1, 0, 2))
    affine = jnp.concatenate([norm_gain.reshape(-1, HD), norm_bias.reshape(-1, HD)])
    entries = jnp.broadcast_to(page_table.reshape(-1, 1), (page_table.size, HD))
    notes = jnp.concatenate([segment_ids.reshape(2, HD), entries]) + 1
    notes = jnp.pad(notes, ((0, NOTES - notes.shape[0]), (0, 0))).astype(bf16)

    piece_shapes = [(2 * PAGE + NOTES, HD), (2 * PAGE, HD)] * heads
    normed, *own = pl.pallas_call(
        functools.partial(project_kernel, tp, heads),
        out_shape=[jax.ShapeDtypeStruct((rows, width), bf16)]
        + [jax.ShapeDtypeStruct(shape, bf16) for shape in piece_shapes],
        in_specs=[SMEM] + [HBM] * 2 + [VMEM] * (1 + tp),
        out_specs=[VMEM] * (1 + 2 * heads),
        scratch_shapes=[
            pltpu.VMEM((rows, features), bf16),
            pltpu.VMEM((2, width, local_width), bf16),
            pltpu.VMEM((2, width), jnp.float32),
            pltpu.VMEM((rows, local_width), bf16),
            pltpu.SemaphoreType.DMA((3,)),
        ],
        compiler_params=pltpu.CompilerParams(vmem_limit_bytes=PROJECT_VMEM),
        cost_estimate=cost(4 * rows * width * local_width, 4 * width * local_width),
        name="project",
    )(pack_lengths, tokens, weights, affine, notes, *received)
    pages = [
        jnp.stack([own[page]] + [paired(own[2 * bit + page], "req", bit) for bit in range(1, heads)])
        for page in range(2)
    ]
    queries = pl.pallas_call(
        functools.partial(query_kernel, heads),
        out_shape=[jax.ShapeDtypeStruct((rows, HD), bf16)] * heads,
        in_specs=[VMEM, HBM],
        out_specs=[VMEM] * heads,
        scratch_shapes=[
            pltpu.VMEM((rows, local_width), bf16),
            pltpu.VMEM((width, local_width), bf16),
            pltpu.SemaphoreType.DMA,
        ],
        compiler_params=pltpu.CompilerParams(vmem_limit_bytes=24 << 20),
        cost_estimate=cost(2 * rows * width * local_width, 2 * width * local_width),
        name="queries",
    )(normed, weights)
    pages[0], queries = lax.optimization_barrier((pages[0], queries))
    layers = [pages]
    queries = [queries[0]] + [paired(queries[bit], "req", bit) for bit in range(1, heads)]

    def ahead(buffer):
        return forward(buffer, "req", heads)

    layers.append([ahead(buffer) for buffer in layers[0]])

    state_shape = [
        jax.ShapeDtypeStruct((heads, rows, HD), jnp.float32),
        jax.ShapeDtypeStruct((heads, rows, 2 * HD), jnp.float32),
    ]

    def attend(tiles, state, last, cache_page):
        pairs = heads * rows * heads * PAGE * len(tiles)
        operands = (
            list(queries)
            + [layers[layer][0] for layer in noted_layers(reach, tiles, cache_page)]
            + [layers[layer][page] for layer, page in page_list(reach, tiles, cache_page)]
            + list(state)
        )
        if last:
            outs = [jax.ShapeDtypeStruct((rows + 2 * PAGE, HD), bf16)] * heads
        else:
            outs = ([] if state else state_shape[:1]) + state_shape + (
                [jax.ShapeDtypeStruct((2 * PAGE, HD), bf16)] * heads
                if cache_page is not None
                else []
            )
        return pl.pallas_call(
            functools.partial(
                attend_kernel, heads, reach, packs, tiles, not state, last, cache_page
            ),
            out_shape=outs,
            in_specs=[VMEM] * len(operands),
            out_specs=[VMEM] * len(outs),
            compiler_params=pltpu.CompilerParams(vmem_limit_bytes=32 << 20),
            cost_estimate=cost(6 * pairs * HD, 4 << 20, pairs),
            name="attend",
        )(*operands)

    ids, *state = attend([(0, 0), (0, 1)], [], False, None)
    first_page = layers[1][0]
    second_page, state = lax.optimization_barrier((layers[1][1], state))
    for _ in range(1, reach):
        first_page, second_page = ahead(first_page), ahead(second_page)
        layers.append([first_page, second_page])
    for layer in range(1, reach):
        state = attend([(layer, 0), (layer, 1)], [ids, *state], False, None)
    early = pl.pallas_call(
        functools.partial(select_kernel, heads, reach),
        out_shape=[jax.ShapeDtypeStruct((2 * PAGE, HD), bf16)] * heads,
        in_specs=[VMEM] * (reach + 1),
        out_specs=[VMEM] * heads,
        compiler_params=pltpu.CompilerParams(vmem_limit_bytes=8 << 20),
        cost_estimate=cost(0, 1 << 20),
        name="select",
    )(*[layer[0] for layer in layers])
    early = [early[0]] + [paired(early[bit], "req", bit) for bit in range(1, heads)]
    final = attend([(reach, 0), (reach, 1)], [ids, *state], True, 1)
    final, near = lax.optimization_barrier((final, early[:-1]))
    early = near + early[-1:]
    final = [final[0]] + [paired(final[bit], "req", bit) for bit in range(1, heads)]

    context, cache = pl.pallas_call(
        functools.partial(finish_kernel, heads),
        out_shape=[
            jax.ShapeDtypeStruct((rows, local_width), bf16),
            jax.ShapeDtypeStruct((4, 2, PAGE, local_width), bf16),
        ],
        in_specs=[HBM, SMEM] + [VMEM] * (4 * heads),
        out_specs=[VMEM] * 2,
        scratch_shapes=[pltpu.SMEM((2, 2), jnp.int32), pltpu.SemaphoreType.DMA],
        compiler_params=pltpu.CompilerParams(vmem_limit_bytes=16 << 20),
        name="finish",
    )(page_table, pack_lengths, *final, *early, *own)
    return context, cache


def solution(mesh):
    return jax.shard_map(
        per_device,
        mesh=mesh,
        in_specs=(P("req", "tp"), P(), P(), P(None, None, "tp"), P("req"), P(), P("req", None)),
        out_specs=(P("req", "tp"), P("req", None, None, "tp")),
        check_vma=False,
    )
```

```python
import functools
import jax
import jax.numpy as jnp
from jax import lax
from jax.experimental import pallas as pl
from jax.experimental.pallas import tpu as pltpu
from jax.sharding import PartitionSpec as P

HD = 128
PAGE = 128
REACH = 8
NOTES = 16
LIMIT_ROW = 6
MASKED = -1e30
PROJECT_VMEM = 48 << 20
VMEM = pl.BlockSpec(memory_space=pltpu.VMEM)
SMEM = pl.BlockSpec(memory_space=pltpu.SMEM)
HBM = pl.BlockSpec(memory_space=pltpu.HBM)


def paired(shard, axis, bit):
    devices = lax.axis_size(axis)
    return lax.ppermute(shard, axis, [(i, i ^ bit) for i in range(devices)])


def forward(shard, axis, by):
    devices = lax.axis_size(axis)
    return lax.ppermute(shard, axis, [(i, i + by) for i in range(devices - by)])


def cost(flops, moved, transcendentals=0):
    return pl.CostEstimate(flops=flops, bytes_accessed=moved, transcendentals=transcendentals)


def keep_kernel(tokens_ref, kept_ref):
    kept_ref[...] = tokens_ref[...]


def below_limit(notes, row_count):
    rows = lax.broadcasted_iota(jnp.int32, (row_count, HD), 0)
    return rows.astype(jnp.float32) < notes[LIMIT_ROW : LIMIT_ROW + 1]


def project_kernel(tp, heads, *refs):
    refs = list(refs)
    take = lambda count: [refs.pop(0) for _ in range(count)]
    lengths_ref, tokens_ref, w_hbm, table_ref = take(4)
    received, (normed_ref,), pieces = take(tp - 1), take(1), take(2 * heads)
    w_ref, spread_ref, columns, sems = refs
    rows, features = tokens_ref.shape
    here = lax.axis_index("tp")
    me = lax.axis_index("req") % heads
    loads = [
        pltpu.make_async_copy(w_hbm.at[1 + which], w_ref.at[which], sems.at[which])
        for which in range(2)
    ]
    for load in loads:
        load.start()
    notes = table_ref[:NOTES, :] + 1.0
    affine = table_ref[NOTES:, :]
    lines = affine.shape[0] // 2
    for row in range(2):
        for line in range(lines):
            spread_ref[row : row + 1, line * HD : (line + 1) * HD] = affine[
                row * lines + line : row * lines + line + 1
            ]
    parts = [tokens_ref] + received
    step = 32

    def norm_rows(index, carry):
        at = pl.ds(pl.multiple_of(index * step, step), step)
        shares = [part[at, :].astype(jnp.float32) for part in parts]
        total = sum(jnp.sum(share, axis=1, keepdims=True) for share in shares)
        mean = total * (1.0 / (tp * features))
        centred = [share - mean for share in shares]
        squares = sum(jnp.sum(share * share, axis=1, keepdims=True) for share in centred)
        scale = lax.rsqrt(squares * (1.0 / (tp * features)) + 1e-05)
        for bit, share in enumerate(centred):
            lanes = pl.ds(pl.multiple_of((here ^ bit) * features, features), features)
            gain = spread_ref[0:1, lanes]
            bias = spread_ref[1:2, lanes]
            normed_ref[at, lanes] = (share * scale * gain + bias).astype(jnp.bfloat16)
        return carry

    lax.fori_loop(0, rows // step, norm_rows, 0)

    device = lax.axis_index("req")
    per_pack = lax.axis_size("req") // lengths_ref.shape[0]
    limit = lengths_ref[device // per_pack] - device % per_pack * rows
    limit = jnp.clip(limit, 0, rows).astype(jnp.float32)
    row = lax.broadcasted_iota(jnp.int32, notes.shape, 0)
    entries = [notes[2 + page : 3 + page, at : at + 1] for page in range(2) for at in range(2)]
    for at, entry in enumerate(entries):
        notes = jnp.where(row == 2 + at, entry, notes)
    notes = jnp.where(row == LIMIT_ROW, limit, notes)
    valid = below_limit(notes, rows)
    notes = notes.astype(jnp.bfloat16)
    for which in range(2):
        loads[which].wait()
        projected = jnp.dot(normed_ref[...], w_ref[which], preferred_element_type=jnp.float32)
        columns[...] = jnp.where(valid[:, :1], projected, 0.0).astype(jnp.bfloat16)
        for bit in range(heads):
            lanes = pl.ds(pl.multiple_of((me ^ bit) * HD, HD), HD)
            for page in range(2):
                pieces[2 * bit + page][which * PAGE : (which + 1) * PAGE, :] = columns[
                    page * PAGE : (page + 1) * PAGE, lanes
                ]

    for bit in range(heads):
        pieces[2 * bit][2 * PAGE :, :] = notes


def query_kernel(heads, normed_ref, w_hbm, *refs):
    pieces, (columns, w_ref, sem) = refs[:heads], refs[heads:]
    load = pltpu.make_async_copy(w_hbm.at[0], w_ref, sem)
    load.start()
    load.wait()
    me = lax.axis_index("req") % heads
    projected = jnp.dot(normed_ref[...], w_ref[...], preferred_element_type=jnp.float32)
    columns[...] = (projected * HD ** (-0.5)).astype(jnp.bfloat16)
    for bit in range(heads):
        pieces[bit][...] = columns[:, pl.ds(pl.multiple_of((me ^ bit) * HD, HD), HD)]


def attend_kernel(heads, reach, packs, tiles, first, last, cache_page, *refs):
    refs = list(refs)
    take = lambda count: [refs.pop(0) for _ in range(count)]
    queries = take(heads)
    noted = dict(zip(noted_layers(reach, tiles, cache_page), take(len(noted_layers(reach, tiles, cache_page)))))
    pages = dict(zip(page_list(reach, tiles, cache_page), take(len(page_list(reach, tiles, cache_page)))))
    pages.update({(layer, 0): buffer for layer, buffer in noted.items()})
    ids_ref, top_ref, total_ref = (None,) * 3 if first else take(3)
    if first:
        ids_ref = take(1)[0]
    top_out, total_out = (None,) * 2 if last else take(2)
    outs = refs
    device = lax.axis_index("req")
    per_pack = lax.axis_size("req") // packs
    me = device % heads
    rows = 2 * PAGE
    width = heads * PAGE
    notes = {
        layer: [buffer[bit, 2 * PAGE :, :].astype(jnp.float32) for bit in range(heads)]
        for layer, buffer in noted.items()
    }
    keys, values, key_ids, key_places = [], [], [], []
    ones = jnp.ones((width, HD), jnp.bfloat16)
    lane = lax.broadcasted_iota(jnp.int32, (1, PAGE), 1)
    for layer, page in tiles:
        buffer = pages[layer, page]
        keys.append(buffer[:, :PAGE].reshape(width, HD))
        values.append(
            jnp.concatenate([buffer[:, PAGE : 2 * PAGE].reshape(width, HD), ones], axis=1)
        )
        ids = jnp.concatenate([note[page : page + 1] for note in notes[layer]], axis=1)
        if layer > 0:
            same_pack = (device - layer * heads) // per_pack == device // per_pack
            ids = jnp.where(same_pack, ids, 0.0)
        key_ids.append(ids)
        key_places.append(
            jnp.concatenate(
                [lane + ((me ^ bit) * rows + page * PAGE) for bit in range(heads)], axis=1
            )
        )
    wide = (PAGE, HD)
    for bit in range(heads):
        for page in range(2):
            at = pl.ds(page * PAGE, PAGE)
            query = queries[bit][at, :]
            if first:
                query_ids = jnp.broadcast_to(notes[0][bit][page : page + 1], wide).T
                ids_ref[bit, at] = query_ids
                place = lax.broadcasted_iota(jnp.int32, wide, 0) + ((me ^ bit) * rows + page * PAGE)
                top = jnp.full(wide, MASKED, jnp.float32)
                total = [jnp.zeros(wide, jnp.float32)] * 2
            else:
                query_ids = ids_ref[bit, at]
                top = top_ref[bit, at]
                total = [total_ref[bit, at, half * HD : (half + 1) * HD] for half in range(2)]
            for index, (layer, _) in enumerate(tiles):
                scores = lax.dot_general(
                    query, keys[index], (((1,), (1,)), ((), ())), preferred_element_type=jnp.float32
                )
                chunks = []
                for other in range(heads):
                    lanes = slice(other * PAGE, (other + 1) * PAGE)
                    allowed = key_ids[index][:, lanes] == query_ids
                    if layer == 0:
                        allowed = allowed & (key_places[index][:, lanes] <= place)
                    chunks.append(jnp.where(allowed, scores[:, lanes], MASKED))
                highest = jnp.max(functools.reduce(jnp.maximum, chunks), axis=1, keepdims=True)
                higher = jnp.maximum(top, jnp.broadcast_to(highest, wide))
                weights = jnp.concatenate(
                    [jnp.exp(chunk - higher).astype(jnp.bfloat16) for chunk in chunks], axis=1
                )
                shrink = jnp.exp(top - higher)
                added = jnp.dot(weights, values[index], preferred_element_type=jnp.float32)
                total = [total[half] * shrink + added[:, half * HD : (half + 1) * HD] for half in range(2)]
                top = higher
            if last:
                outs[bit][at, :] = (total[0] / total[1]).astype(jnp.bfloat16)
            else:
                top_out[bit, at] = top
                for half in range(2):
                    total_out[bit, at, half * HD : (half + 1) * HD] = total[half]
    if cache_page is not None:
        select_pages(heads, reach, cache_page, device, notes, pages, outs, rows)


def select_pages(heads, reach, page, device, notes, pages, outs, start):
    me = device % heads
    sought = jnp.zeros((1, HD), jnp.int32)
    for bit in range(heads):
        owner = ((device ^ bit) + 1).astype(jnp.float32)
        for layer in range(reach + 1):
            for other in range(heads):
                if layer == 0 and other == bit:
                    continue
                note = notes[layer][other]
                at = 2 + 2 * page
                hit = (note[at : at + 1] == owner) & (note[at + 1 : at + 2] == page + 1.0)
                place = (layer * heads + other + 1) << (6 * bit)
                sought = sought | jnp.where(hit, place, 0)
    sought = jnp.max(sought)
    for bit in range(heads):
        found = ((sought >> (6 * bit)) & 63) - 1
        for layer in range(reach + 1):

            @pl.when((found >= layer * heads) & (found < (layer + 1) * heads))
            def _():
                outs[bit][start : start + 2 * PAGE, :] = pages[layer, page][
                    found - layer * heads, : 2 * PAGE, :
                ]

        @pl.when(found < 0)
        def _():
            outs[bit][start : start + 2 * PAGE, :] = jnp.zeros((2 * PAGE, HD), jnp.bfloat16)


def select_kernel(heads, reach, *refs):
    buffers, outs = refs[: reach + 1], refs[reach + 1 :]
    notes = [
        [buffer[bit, 2 * PAGE :, :].astype(jnp.float32) for bit in range(heads)]
        for buffer in buffers
    ]
    pages = {(layer, 0): buffer for layer, buffer in enumerate(buffers)}
    select_pages(heads, reach, 0, lax.axis_index("req"), notes, pages, outs, 0)


def noted_layers(reach, tiles, cache_page):
    layers = range(reach + 1) if cache_page is not None else [0] + [layer for layer, _ in tiles]
    return sorted(set(layers))


def page_list(reach, tiles, cache_page):
    wanted = list(tiles)
    if cache_page is not None:
        wanted += [(layer, cache_page) for layer in range(reach + 1)]
    return sorted(set(place for place in wanted if place[1] == 1))


def finish_kernel(heads, *refs):
    refs = list(refs)
    take = lambda count: [refs.pop(0) for _ in range(count)]
    final, early, own = take(heads), take(heads), take(2 * heads)
    context_ref, cache_ref = refs
    device = lax.axis_index("req")
    me = device % heads
    rows = context_ref.shape[0]
    notes = own[0][2 * PAGE :, :].astype(jnp.float32)
    valid = below_limit(notes, rows)
    here = (device + 1).astype(jnp.float32)
    stays = [
        (notes[2 + 2 * page : 3 + 2 * page] == here)
        & (notes[3 + 2 * page : 4 + 2 * page] == page + 3.0)
        for page in range(2)
    ]
    for bit in range(heads):
        lanes = pl.ds(pl.multiple_of((me ^ bit) * HD, HD), HD)
        context = final[bit][0:rows, :].astype(jnp.float32)
        context_ref[:, lanes] = jnp.where(valid, context, 0.0).astype(jnp.bfloat16)
        for part in range(2):
            first = part * PAGE
            cache_ref[0, part, :, lanes] = early[bit][first : first + PAGE, :]
            cache_ref[1, part, :, lanes] = final[bit][rows + first : rows + first + PAGE, :]
            for page in range(2):
                kept = own[2 * bit + page][first : first + PAGE, :].astype(jnp.float32)
                cache_ref[2 + page, part, :, lanes] = jnp.where(stays[page], kept, 0.0).astype(
                    jnp.bfloat16
                )


def per_device(tokens, norm_gain, norm_bias, w_qkv, segment_ids, pack_lengths, page_table):
    rows, features = tokens.shape
    tp = lax.axis_size("tp")
    local_width = w_qkv.shape[2]
    heads = local_width // HD
    reach = REACH // heads
    width = w_qkv.shape[0]
    packs = pack_lengths.shape[0]
    bf16 = jnp.bfloat16

    received = [paired(tokens, "tp", bit) for bit in range(1, tp)]
    weights = jnp.transpose(w_qkv, (1, 0, 2))
    lines = width // HD

    def placed(entries, row):
        below = NOTES + 2 * lines - row - entries.shape[0]
        return jnp.pad(entries, ((row, below), (0, HD - entries.shape[1])))

    ids, gain, bias = lax.optimization_barrier(
        (
            segment_ids.reshape(2, HD),
            norm_gain.reshape(lines, HD),
            norm_bias.reshape(lines, HD),
        )
    )
    integers = placed(ids, 0) + placed(page_table, 2)
    affine = placed(gain, NOTES) + placed(bias, NOTES + lines)
    table = integers.astype(jnp.float32) + affine.astype(jnp.float32)
    kept = pl.pallas_call(
        keep_kernel,
        out_shape=jax.ShapeDtypeStruct((rows, features), bf16),
        in_specs=[VMEM],
        out_specs=VMEM,
        compiler_params=pltpu.CompilerParams(vmem_limit_bytes=4 << 20),
        cost_estimate=cost(rows * features, 2 * rows * features),
        name="keep",
    )(tokens)

    piece_shapes = [(2 * PAGE + NOTES, HD), (2 * PAGE, HD)] * heads
    normed, *own = pl.pallas_call(
        functools.partial(project_kernel, tp, heads),
        out_shape=[jax.ShapeDtypeStruct((rows, width), bf16)]
        + [jax.ShapeDtypeStruct(shape, bf16) for shape in piece_shapes],
        in_specs=[SMEM, VMEM, HBM] + [VMEM] * tp,
        out_specs=[VMEM] * (1 + 2 * heads),
        scratch_shapes=[
            pltpu.VMEM((2, width, local_width), bf16),
            pltpu.VMEM((2, width), jnp.float32),
            pltpu.VMEM((rows, local_width), bf16),
            pltpu.SemaphoreType.DMA((2,)),
        ],
        compiler_params=pltpu.CompilerParams(vmem_limit_bytes=PROJECT_VMEM),
        cost_estimate=cost(4 * rows * width * local_width, 4 * width * local_width),
        name="project",
    )(pack_lengths, kept, weights, table, *received)
    pages = [
        jnp.stack([own[page]] + [paired(own[2 * bit + page], "req", bit) for bit in range(1, heads)])
        for page in range(2)
    ]
    queries = pl.pallas_call(
        functools.partial(query_kernel, heads),
        out_shape=[jax.ShapeDtypeStruct((rows, HD), bf16)] * heads,
        in_specs=[VMEM, HBM],
        out_specs=[VMEM] * heads,
        scratch_shapes=[
            pltpu.VMEM((rows, local_width), bf16),
            pltpu.VMEM((width, local_width), bf16),
            pltpu.SemaphoreType.DMA,
        ],
        compiler_params=pltpu.CompilerParams(vmem_limit_bytes=24 << 20),
        cost_estimate=cost(2 * rows * width * local_width, 2 * width * local_width),
        name="queries",
    )(normed, weights)
    layers = [pages]
    queries = [queries[0]] + [paired(queries[bit], "req", bit) for bit in range(1, heads)]

    def ahead(buffer):
        return forward(buffer, "req", heads)

    layers.append([ahead(buffer) for buffer in layers[0]])

    state_shape = [
        jax.ShapeDtypeStruct((heads, rows, HD), jnp.float32),
        jax.ShapeDtypeStruct((heads, rows, 2 * HD), jnp.float32),
    ]

    def attend(tiles, state, last, cache_page):
        pairs = heads * rows * heads * PAGE * len(tiles)
        operands = (
            list(queries)
            + [layers[layer][0] for layer in noted_layers(reach, tiles, cache_page)]
            + [layers[layer][page] for layer, page in page_list(reach, tiles, cache_page)]
            + list(state)
        )
        if last:
            outs = [jax.ShapeDtypeStruct((rows + 2 * PAGE, HD), bf16)] * heads
        else:
            outs = ([] if state else state_shape[:1]) + state_shape + (
                [jax.ShapeDtypeStruct((2 * PAGE, HD), bf16)] * heads
                if cache_page is not None
                else []
            )
        return pl.pallas_call(
            functools.partial(
                attend_kernel, heads, reach, packs, tiles, not state, last, cache_page
            ),
            out_shape=outs,
            in_specs=[VMEM] * len(operands),
            out_specs=[VMEM] * len(outs),
            compiler_params=pltpu.CompilerParams(vmem_limit_bytes=32 << 20),
            cost_estimate=cost(6 * pairs * HD, 4 << 20, pairs),
            name="attend",
        )(*operands)

    ids, *state = attend([(0, 0), (0, 1)], [], False, None)
    first_page = layers[1][0]
    second_page, state = lax.optimization_barrier((layers[1][1], state))
    for _ in range(1, reach):
        first_page, second_page = ahead(first_page), ahead(second_page)
        layers.append([first_page, second_page])
    for layer in range(1, reach):
        state = attend([(layer, 0), (layer, 1)], [ids, *state], False, None)
    early = pl.pallas_call(
        functools.partial(select_kernel, heads, reach),
        out_shape=[jax.ShapeDtypeStruct((2 * PAGE, HD), bf16)] * heads,
        in_specs=[VMEM] * (reach + 1),
        out_specs=[VMEM] * heads,
        compiler_params=pltpu.CompilerParams(vmem_limit_bytes=8 << 20),
        cost_estimate=cost(0, 1 << 20),
        name="select",
    )(*[layer[0] for layer in layers])
    early = [early[0]] + [paired(early[bit], "req", bit) for bit in range(1, heads)]
    final = list(attend([(reach, 0), (reach, 1)], [ids, *state], True, 1))
    for bit in range(1, heads):
        final[bit], early[bit] = lax.optimization_barrier((final[bit], early[bit]))
    final = [final[0]] + [paired(final[bit], "req", bit) for bit in range(1, heads)]

    context, cache = pl.pallas_call(
        functools.partial(finish_kernel, heads),
        out_shape=[
            jax.ShapeDtypeStruct((rows, local_width), bf16),
            jax.ShapeDtypeStruct((4, 2, PAGE, local_width), bf16),
        ],
        in_specs=[VMEM] * (4 * heads),
        out_specs=[VMEM] * 2,
        compiler_params=pltpu.CompilerParams(vmem_limit_bytes=16 << 20),
        name="finish",
    )(*final, *early, *own)
    return context, cache


def solution(mesh):
    return jax.shard_map(
        per_device,
        mesh=mesh,
        in_specs=(P("req", "tp"), P(), P(), P(None, None, "tp"), P("req"), P(), P("req", None)),
        out_specs=(P("req", "tp"), P("req", None, None, "tp")),
        check_vma=False,
    )
```

```python
import functools
import jax
import jax.numpy as jnp
from jax import lax
from jax.experimental import pallas as pl
from jax.experimental.pallas import tpu as pltpu
from jax.sharding import PartitionSpec as P

HD = 128
PAGE = 128
REACH = 8
NOTES = 16
LIMIT_ROW = 6
MASKED = -1e30
PROJECT_VMEM = 48 << 20
VMEM = pl.BlockSpec(memory_space=pltpu.VMEM)
SMEM = pl.BlockSpec(memory_space=pltpu.SMEM)
HBM = pl.BlockSpec(memory_space=pltpu.HBM)


def paired(shard, axis, bit):
    devices = lax.axis_size(axis)
    return lax.ppermute(shard, axis, [(i, i ^ bit) for i in range(devices)])


def forward(shard, axis, by):
    devices = lax.axis_size(axis)
    return lax.ppermute(shard, axis, [(i, i + by) for i in range(devices - by)])


def cost(flops, moved, transcendentals=0):
    return pl.CostEstimate(flops=flops, bytes_accessed=moved, transcendentals=transcendentals)


def keep_kernel(tokens_ref, kept_ref):
    kept_ref[...] = tokens_ref[...]


def below_limit(notes, row_count):
    rows = lax.broadcasted_iota(jnp.int32, (row_count, HD), 0)
    return rows.astype(jnp.float32) < notes[LIMIT_ROW : LIMIT_ROW + 1]


def project_kernel(tp, heads, *refs):
    refs = list(refs)
    take = lambda count: [refs.pop(0) for _ in range(count)]
    lengths_ref, tokens_ref, w_hbm, table_ref = take(4)
    received, (normed_ref,), pieces = take(tp - 1), take(1), take(2 * heads)
    w_ref, spread_ref, means_ref, columns, sems = refs
    rows, features = tokens_ref.shape
    here = lax.axis_index("tp")
    me = lax.axis_index("req") % heads
    loads = [
        pltpu.make_async_copy(w_hbm.at[1 + which], w_ref.at[which], sems.at[which])
        for which in range(2)
    ]
    for load in loads:
        load.start()
    notes = table_ref[:NOTES, :] + 1.0
    affine = table_ref[NOTES:, :]
    lines = affine.shape[0] // 2
    for row in range(2):
        for line in range(lines):
            spread_ref[row : row + 1, line * HD : (line + 1) * HD] = affine[
                row * lines + line : row * lines + line + 1
            ]
    parts = [tokens_ref] + received
    ones = jnp.ones((features, HD), jnp.bfloat16)
    share = 1.0 / (tp * features)
    means_ref[...] = share * sum(
        jnp.dot(part[...], ones, preferred_element_type=jnp.float32) for part in parts
    )
    step = 64

    def norm_rows(index, carry):
        at = pl.ds(pl.multiple_of(index * step, step), step)
        mean = means_ref[at, :]
        chunks = [(bit, lane) for bit in range(tp) for lane in range(0, features, HD)]
        squares = jnp.zeros((step, HD), jnp.float32)
        for bit, lane in chunks:
            centred = parts[bit][at, lane : lane + HD].astype(jnp.float32) - mean
            squares = squares + centred * centred
        variance = share * jnp.sum(squares, axis=1, keepdims=True)
        scale = jnp.broadcast_to(lax.rsqrt(variance + 1e-05), (step, HD))
        for bit, lane in chunks:
            lanes = pl.ds(pl.multiple_of((here ^ bit) * features + lane, HD), HD)
            centred = parts[bit][at, lane : lane + HD].astype(jnp.float32) - mean
            normed = centred * scale * spread_ref[0:1, lanes] + spread_ref[1:2, lanes]
            normed_ref[at, lanes] = normed.astype(jnp.bfloat16)
        return carry

    lax.fori_loop(0, rows // step, norm_rows, 0)

    device = lax.axis_index("req")
    per_pack = lax.axis_size("req") // lengths_ref.shape[0]
    limit = lengths_ref[device // per_pack] - device % per_pack * rows
    limit = jnp.clip(limit, 0, rows).astype(jnp.float32)
    row = lax.broadcasted_iota(jnp.int32, notes.shape, 0)
    entries = [notes[2 + page : 3 + page, at : at + 1] for page in range(2) for at in range(2)]
    for at, entry in enumerate(entries):
        notes = jnp.where(row == 2 + at, entry, notes)
    notes = jnp.where(row == LIMIT_ROW, limit, notes)
    valid = below_limit(notes, rows)
    notes = notes.astype(jnp.bfloat16)
    for which in range(2):
        loads[which].wait()
        projected = jnp.dot(normed_ref[...], w_ref[which], preferred_element_type=jnp.float32)
        columns[...] = jnp.where(valid[:, :1], projected, 0.0).astype(jnp.bfloat16)
        for bit in range(heads):
            lanes = pl.ds(pl.multiple_of((me ^ bit) * HD, HD), HD)
            for page in range(2):
                pieces[2 * bit + page][which * PAGE : (which + 1) * PAGE, :] = columns[
                    page * PAGE : (page + 1) * PAGE, lanes
                ]

    for bit in range(heads):
        pieces[2 * bit][2 * PAGE :, :] = notes


def query_kernel(heads, normed_ref, w_hbm, *refs):
    pieces, (columns, w_ref, sem) = refs[:heads], refs[heads:]
    load = pltpu.make_async_copy(w_hbm.at[0], w_ref, sem)
    load.start()
    load.wait()
    me = lax.axis_index("req") % heads
    projected = jnp.dot(normed_ref[...], w_ref[...], preferred_element_type=jnp.float32)
    columns[...] = (projected * HD ** (-0.5)).astype(jnp.bfloat16)
    for bit in range(heads):
        pieces[bit][...] = columns[:, pl.ds(pl.multiple_of((me ^ bit) * HD, HD), HD)]


def attend_kernel(heads, reach, packs, tiles, first, last, cache_page, *refs):
    refs = list(refs)
    take = lambda count: [refs.pop(0) for _ in range(count)]
    queries = take(heads)
    noted = dict(zip(noted_layers(reach, tiles, cache_page), take(len(noted_layers(reach, tiles, cache_page)))))
    pages = dict(zip(page_list(reach, tiles, cache_page), take(len(page_list(reach, tiles, cache_page)))))
    pages.update({(layer, 0): buffer for layer, buffer in noted.items()})
    ids_ref, top_ref, total_ref = (None,) * 3 if first else take(3)
    if first:
        ids_ref = take(1)[0]
    top_out, total_out = (None,) * 2 if last else take(2)
    outs = refs
    device = lax.axis_index("req")
    per_pack = lax.axis_size("req") // packs
    me = device % heads
    rows = 2 * PAGE
    width = heads * PAGE
    notes = {
        layer: [buffer[bit, 2 * PAGE :, :].astype(jnp.float32) for bit in range(heads)]
        for layer, buffer in noted.items()
    }
    keys, values, key_ids, key_places = [], [], [], []
    ones = jnp.ones((width, HD), jnp.bfloat16)
    lane = lax.broadcasted_iota(jnp.int32, (1, PAGE), 1)
    for layer, page in tiles:
        buffer = pages[layer, page]
        keys.append(buffer[:, :PAGE].reshape(width, HD))
        values.append(
            jnp.concatenate([buffer[:, PAGE : 2 * PAGE].reshape(width, HD), ones], axis=1)
        )
        ids = jnp.concatenate([note[page : page + 1] for note in notes[layer]], axis=1)
        if layer > 0:
            same_pack = (device - layer * heads) // per_pack == device // per_pack
            ids = jnp.where(same_pack, ids, 0.0)
        key_ids.append(ids)
        key_places.append(
            jnp.concatenate(
                [lane + ((me ^ bit) * rows + page * PAGE) for bit in range(heads)], axis=1
            )
        )
    wide = (PAGE, HD)
    for bit in range(heads):
        for page in range(2):
            at = pl.ds(page * PAGE, PAGE)
            query = queries[bit][at, :]
            if first:
                query_ids = jnp.broadcast_to(notes[0][bit][page : page + 1], wide).T
                ids_ref[bit, at] = query_ids
                place = lax.broadcasted_iota(jnp.int32, wide, 0) + ((me ^ bit) * rows + page * PAGE)
                top = jnp.full(wide, MASKED, jnp.float32)
                total = [jnp.zeros(wide, jnp.float32)] * 2
            else:
                query_ids = ids_ref[bit, at]
                top = top_ref[bit, at]
                total = [total_ref[bit, at, half * HD : (half + 1) * HD] for half in range(2)]
            for index, (layer, _) in enumerate(tiles):
                scores = lax.dot_general(
                    query, keys[index], (((1,), (1,)), ((), ())), preferred_element_type=jnp.float32
                )
                chunks = []
                for other in range(heads):
                    lanes = slice(other * PAGE, (other + 1) * PAGE)
                    allowed = key_ids[index][:, lanes] == query_ids
                    if layer == 0:
                        allowed = allowed & (key_places[index][:, lanes] <= place)
                    chunks.append(jnp.where(allowed, scores[:, lanes], MASKED))
                highest = jnp.max(functools.reduce(jnp.maximum, chunks), axis=1, keepdims=True)
                higher = jnp.maximum(top, jnp.broadcast_to(highest, wide))
                weights = jnp.concatenate(
                    [jnp.exp(chunk - higher).astype(jnp.bfloat16) for chunk in chunks], axis=1
                )
                shrink = jnp.exp(top - higher)
                added = jnp.dot(weights, values[index], preferred_element_type=jnp.float32)
                total = [total[half] * shrink + added[:, half * HD : (half + 1) * HD] for half in range(2)]
                top = higher
            if last:
                outs[bit][at, :] = (total[0] / total[1]).astype(jnp.bfloat16)
            else:
                top_out[bit, at] = top
                for half in range(2):
                    total_out[bit, at, half * HD : (half + 1) * HD] = total[half]
    if cache_page is not None:
        select_pages(heads, reach, cache_page, device, notes, pages, outs, rows)


def select_pages(heads, reach, page, device, notes, pages, outs, start):
    me = device % heads
    sought = jnp.zeros((1, HD), jnp.int32)
    for bit in range(heads):
        owner = ((device ^ bit) + 1).astype(jnp.float32)
        for layer in range(reach + 1):
            for other in range(heads):
                if layer == 0 and other == bit:
                    continue
                note = notes[layer][other]
                at = 2 + 2 * page
                hit = (note[at : at + 1] == owner) & (note[at + 1 : at + 2] == page + 1.0)
                place = (layer * heads + other + 1) << (6 * bit)
                sought = sought | jnp.where(hit, place, 0)
    sought = jnp.max(sought)
    for bit in range(heads):
        found = ((sought >> (6 * bit)) & 63) - 1
        for layer in range(reach + 1):

            @pl.when((found >= layer * heads) & (found < (layer + 1) * heads))
            def _():
                outs[bit][start : start + 2 * PAGE, :] = pages[layer, page][
                    found - layer * heads, : 2 * PAGE, :
                ]

        @pl.when(found < 0)
        def _():
            outs[bit][start : start + 2 * PAGE, :] = jnp.zeros((2 * PAGE, HD), jnp.bfloat16)


def select_kernel(heads, reach, *refs):
    buffers, outs = refs[: reach + 1], refs[reach + 1 :]
    notes = [
        [buffer[bit, 2 * PAGE :, :].astype(jnp.float32) for bit in range(heads)]
        for buffer in buffers
    ]
    pages = {(layer, 0): buffer for layer, buffer in enumerate(buffers)}
    select_pages(heads, reach, 0, lax.axis_index("req"), notes, pages, outs, 0)


def noted_layers(reach, tiles, cache_page):
    layers = range(reach + 1) if cache_page is not None else [0] + [layer for layer, _ in tiles]
    return sorted(set(layers))


def page_list(reach, tiles, cache_page):
    wanted = list(tiles)
    if cache_page is not None:
        wanted += [(layer, cache_page) for layer in range(reach + 1)]
    return sorted(set(place for place in wanted if place[1] == 1))


def finish_kernel(heads, *refs):
    refs = list(refs)
    take = lambda count: [refs.pop(0) for _ in range(count)]
    final, early, own = take(heads), take(heads), take(2 * heads)
    context_ref, cache_ref = refs
    device = lax.axis_index("req")
    me = device % heads
    rows = context_ref.shape[0]
    notes = own[0][2 * PAGE :, :].astype(jnp.float32)
    valid = below_limit(notes, rows)
    here = (device + 1).astype(jnp.float32)
    stays = [
        (notes[2 + 2 * page : 3 + 2 * page] == here)
        & (notes[3 + 2 * page : 4 + 2 * page] == page + 3.0)
        for page in range(2)
    ]
    for bit in range(heads):
        lanes = pl.ds(pl.multiple_of((me ^ bit) * HD, HD), HD)
        context = final[bit][0:rows, :].astype(jnp.float32)
        context_ref[:, lanes] = jnp.where(valid, context, 0.0).astype(jnp.bfloat16)
        for part in range(2):
            first = part * PAGE
            cache_ref[0, part, :, lanes] = early[bit][first : first + PAGE, :]
            cache_ref[1, part, :, lanes] = final[bit][rows + first : rows + first + PAGE, :]
            for page in range(2):
                kept = own[2 * bit + page][first : first + PAGE, :].astype(jnp.float32)
                cache_ref[2 + page, part, :, lanes] = jnp.where(stays[page], kept, 0.0).astype(
                    jnp.bfloat16
                )


def per_device(tokens, norm_gain, norm_bias, w_qkv, segment_ids, pack_lengths, page_table):
    rows, features = tokens.shape
    tp = lax.axis_size("tp")
    local_width = w_qkv.shape[2]
    heads = local_width // HD
    reach = REACH // heads
    width = w_qkv.shape[0]
    packs = pack_lengths.shape[0]
    bf16 = jnp.bfloat16

    received = [paired(tokens, "tp", bit) for bit in range(1, tp)]
    weights = jnp.transpose(w_qkv, (1, 0, 2))
    lines = width // HD

    def placed(entries, row):
        below = NOTES + 2 * lines - row - entries.shape[0]
        return jnp.pad(entries, ((row, below), (0, HD - entries.shape[1])))

    ids, gain, bias = lax.optimization_barrier(
        (
            segment_ids.reshape(2, HD),
            norm_gain.reshape(lines, HD),
            norm_bias.reshape(lines, HD),
        )
    )
    integers = placed(ids, 0) + placed(page_table, 2)
    affine = placed(gain, NOTES) + placed(bias, NOTES + lines)
    table = integers.astype(jnp.float32) + affine.astype(jnp.float32)
    kept = pl.pallas_call(
        keep_kernel,
        out_shape=jax.ShapeDtypeStruct((rows, features), bf16),
        in_specs=[VMEM],
        out_specs=VMEM,
        compiler_params=pltpu.CompilerParams(vmem_limit_bytes=4 << 20),
        cost_estimate=cost(rows * features, 2 * rows * features),
        name="keep",
    )(tokens)

    piece_shapes = [(2 * PAGE + NOTES, HD), (2 * PAGE, HD)] * heads
    normed, *own = pl.pallas_call(
        functools.partial(project_kernel, tp, heads),
        out_shape=[jax.ShapeDtypeStruct((rows, width), bf16)]
        + [jax.ShapeDtypeStruct(shape, bf16) for shape in piece_shapes],
        in_specs=[SMEM, VMEM, HBM] + [VMEM] * tp,
        out_specs=[VMEM] * (1 + 2 * heads),
        scratch_shapes=[
            pltpu.VMEM((2, width, local_width), bf16),
            pltpu.VMEM((2, width), jnp.float32),
            pltpu.VMEM((rows, HD), jnp.float32),
            pltpu.VMEM((rows, local_width), bf16),
            pltpu.SemaphoreType.DMA((2,)),
        ],
        compiler_params=pltpu.CompilerParams(vmem_limit_bytes=PROJECT_VMEM),
        cost_estimate=cost(4 * rows * width * local_width, 4 * width * local_width),
        name="project",
    )(pack_lengths, kept, weights, table, *received)
    pages = [
        jnp.stack([own[page]] + [paired(own[2 * bit + page], "req", bit) for bit in range(1, heads)])
        for page in range(2)
    ]
    queries = pl.pallas_call(
        functools.partial(query_kernel, heads),
        out_shape=[jax.ShapeDtypeStruct((rows, HD), bf16)] * heads,
        in_specs=[VMEM, HBM],
        out_specs=[VMEM] * heads,
        scratch_shapes=[
            pltpu.VMEM((rows, local_width), bf16),
            pltpu.VMEM((width, local_width), bf16),
            pltpu.SemaphoreType.DMA,
        ],
        compiler_params=pltpu.CompilerParams(vmem_limit_bytes=24 << 20),
        cost_estimate=cost(2 * rows * width * local_width, 2 * width * local_width),
        name="queries",
    )(normed, weights)
    layers = [pages]
    queries = [queries[0]] + [paired(queries[bit], "req", bit) for bit in range(1, heads)]

    def ahead(buffer):
        return forward(buffer, "req", heads)

    layers.append([ahead(buffer) for buffer in layers[0]])

    state_shape = [
        jax.ShapeDtypeStruct((heads, rows, HD), jnp.float32),
        jax.ShapeDtypeStruct((heads, rows, 2 * HD), jnp.float32),
    ]

    def attend(tiles, state, last, cache_page):
        pairs = heads * rows * heads * PAGE * len(tiles)
        operands = (
            list(queries)
            + [layers[layer][0] for layer in noted_layers(reach, tiles, cache_page)]
            + [layers[layer][page] for layer, page in page_list(reach, tiles, cache_page)]
            + list(state)
        )
        if last:
            outs = [jax.ShapeDtypeStruct((rows + 2 * PAGE, HD), bf16)] * heads
        else:
            outs = ([] if state else state_shape[:1]) + state_shape + (
                [jax.ShapeDtypeStruct((2 * PAGE, HD), bf16)] * heads
                if cache_page is not None
                else []
            )
        return pl.pallas_call(
            functools.partial(
                attend_kernel, heads, reach, packs, tiles, not state, last, cache_page
            ),
            out_shape=outs,
            in_specs=[VMEM] * len(operands),
            out_specs=[VMEM] * len(outs),
            compiler_params=pltpu.CompilerParams(vmem_limit_bytes=32 << 20),
            cost_estimate=cost(6 * pairs * HD, 4 << 20, pairs),
            name="attend",
        )(*operands)

    ids, *state = attend([(0, 0), (0, 1)], [], False, None)
    first_page = layers[1][0]
    second_page, state = lax.optimization_barrier((layers[1][1], state))
    for _ in range(1, reach):
        first_page, second_page = ahead(first_page), ahead(second_page)
        layers.append([first_page, second_page])
    for layer in range(1, reach):
        state = attend([(layer, 0), (layer, 1)], [ids, *state], False, None)
    early = pl.pallas_call(
        functools.partial(select_kernel, heads, reach),
        out_shape=[jax.ShapeDtypeStruct((2 * PAGE, HD), bf16)] * heads,
        in_specs=[VMEM] * (reach + 1),
        out_specs=[VMEM] * heads,
        compiler_params=pltpu.CompilerParams(vmem_limit_bytes=8 << 20),
        cost_estimate=cost(0, 1 << 20),
        name="select",
    )(*[layer[0] for layer in layers])
    early = [early[0]] + [paired(early[bit], "req", bit) for bit in range(1, heads)]
    final = list(attend([(reach, 0), (reach, 1)], [ids, *state], True, 1))
    for bit in range(1, heads):
        final[bit], early[1 : bit + 1] = lax.optimization_barrier((final[bit], early[1 : bit + 1]))
    final = [final[0]] + [paired(final[bit], "req", bit) for bit in range(1, heads)]

    context, cache = pl.pallas_call(
        functools.partial(finish_kernel, heads),
        out_shape=[
            jax.ShapeDtypeStruct((rows, local_width), bf16),
            jax.ShapeDtypeStruct((4, 2, PAGE, local_width), bf16),
        ],
        in_specs=[VMEM] * (4 * heads),
        out_specs=[VMEM] * 2,
        compiler_params=pltpu.CompilerParams(vmem_limit_bytes=16 << 20),
        name="finish",
    )(*final, *early, *own)
    return context, cache


def solution(mesh):
    return jax.shard_map(
        per_device,
        mesh=mesh,
        in_specs=(P("req", "tp"), P(), P(), P(None, None, "tp"), P("req"), P(), P("req", None)),
        out_specs=(P("req", "tp"), P("req", None, None, "tp")),
        check_vma=False,
    )
```

```python
import functools
import jax
import jax.numpy as jnp
from jax import lax
from jax.experimental import pallas as pl
from jax.experimental.pallas import tpu as pltpu
from jax.sharding import PartitionSpec as P

HD = 128
PAGE = 128
REACH = 8
NOTES = 16
MASKED = -1e30
PROJECT_VMEM = 48 << 20
VMEM = pl.BlockSpec(memory_space=pltpu.VMEM)
SMEM = pl.BlockSpec(memory_space=pltpu.SMEM)
HBM = pl.BlockSpec(memory_space=pltpu.HBM)


def paired(shard, axis, bit):
    devices = lax.axis_size(axis)
    return lax.ppermute(shard, axis, [(i, i ^ bit) for i in range(devices)])


def forward(shard, axis, by):
    devices = lax.axis_size(axis)
    return lax.ppermute(shard, axis, [(i, i + by) for i in range(devices - by)])


def cost(flops, moved, transcendentals=0):
    return pl.CostEstimate(flops=flops, bytes_accessed=moved, transcendentals=transcendentals)


def keep_kernel(tokens_ref, kept_ref):
    kept_ref[...] = tokens_ref[...]


def move(distance, slot):
    return 4 * distance + slot + 1


def project_kernel(tp, heads, *refs):
    refs = list(refs)
    take = lambda count: [refs.pop(0) for _ in range(count)]
    lengths_ref, tokens_ref, w_hbm, table_ref = take(4)
    received, (normed_ref, valid_ref), pieces = take(tp - 1), take(2), take(2 * heads)
    w_ref, spread_ref, means_ref, columns, sems = refs
    rows, features = tokens_ref.shape
    here = lax.axis_index("tp")
    me = lax.axis_index("req") % heads
    loads = [
        pltpu.make_async_copy(w_hbm.at[1 + which], w_ref.at[which], sems.at[which])
        for which in range(2)
    ]
    for load in loads:
        load.start()
    affine = table_ref[NOTES:, :]
    lines = affine.shape[0] // 2
    for row in range(2):
        for line in range(lines):
            spread_ref[row : row + 1, line * HD : (line + 1) * HD] = affine[
                row * lines + line : row * lines + line + 1
            ]
    parts = [tokens_ref] + received
    ones = jnp.ones((features, HD), jnp.bfloat16)
    share = 1.0 / (tp * features)
    means_ref[...] = share * sum(
        jnp.dot(part[...], ones, preferred_element_type=jnp.float32) for part in parts
    )
    step = 64

    def norm_rows(index, carry):
        at = pl.ds(pl.multiple_of(index * step, step), step)
        mean = means_ref[at, :]
        chunks = [(bit, lane) for bit in range(tp) for lane in range(0, features, HD)]
        squares = jnp.zeros((step, HD), jnp.float32)
        for bit, lane in chunks:
            centred = parts[bit][at, lane : lane + HD].astype(jnp.float32) - mean
            squares = squares + centred * centred
        variance = share * jnp.sum(squares, axis=1, keepdims=True)
        scale = jnp.broadcast_to(lax.rsqrt(variance + 1e-05), (step, HD))
        for bit, lane in chunks:
            lanes = pl.ds(pl.multiple_of((here ^ bit) * features + lane, HD), HD)
            centred = parts[bit][at, lane : lane + HD].astype(jnp.float32) - mean
            normed = centred * scale * spread_ref[0:1, lanes] + spread_ref[1:2, lanes]
            normed_ref[at, lanes] = normed.astype(jnp.bfloat16)
        return carry

    lax.fori_loop(0, rows // step, norm_rows, 0)

    device = lax.axis_index("req")
    per_pack = lax.axis_size("req") // lengths_ref.shape[0]
    limit = lengths_ref[device // per_pack] - device % per_pack * rows
    valid = lax.broadcasted_iota(jnp.int32, (rows, HD), 0) < limit
    valid_ref[...] = valid.astype(jnp.float32)
    row = lax.broadcasted_iota(jnp.int32, (NOTES, HD), 0)
    notes = jnp.zeros((NOTES, HD), jnp.float32)
    for page in range(2):
        entry = table_ref[2 + page : 3 + page, :]
        way = move(entry[:, 0:1] - device.astype(jnp.float32), entry[:, 1:2])
        notes = jnp.where(row % 4 == page, table_ref[page : page + 1, :] + 1.0, notes)
        notes = jnp.where(row % 4 == 2 + page, way, notes)
    for which in range(2):
        loads[which].wait()
        projected = jnp.dot(normed_ref[...], w_ref[which], preferred_element_type=jnp.float32)
        columns[...] = jnp.where(valid[:, :1], projected, 0.0).astype(jnp.bfloat16)
        for bit in range(heads):
            lanes = pl.ds(pl.multiple_of((me ^ bit) * HD, HD), HD)
            for page in range(2):
                pieces[2 * bit + page][which * PAGE : (which + 1) * PAGE, :] = columns[
                    page * PAGE : (page + 1) * PAGE, lanes
                ]

    for bit in range(heads):
        kept = jnp.where(row // 4 == bit, notes, 0.0)
        pieces[2 * bit][2 * PAGE :, :] = kept.astype(jnp.bfloat16)


def query_kernel(heads, normed_ref, w_hbm, *refs):
    pieces, (columns, w_ref, sem) = refs[:heads], refs[heads:]
    load = pltpu.make_async_copy(w_hbm.at[0], w_ref, sem)
    load.start()
    load.wait()
    me = lax.axis_index("req") % heads
    projected = jnp.dot(normed_ref[...], w_ref[...], preferred_element_type=jnp.float32)
    columns[...] = (projected * HD ** (-0.5)).astype(jnp.bfloat16)
    for bit in range(heads):
        pieces[bit][...] = columns[:, pl.ds(pl.multiple_of((me ^ bit) * HD, HD), HD)]


def attend_kernel(heads, reach, packs, tiles, first, last, cache_page, *refs):
    refs = list(refs)
    take = lambda count: [refs.pop(0) for _ in range(count)]
    queries = take(heads)
    noted = dict(zip(noted_layers(reach, tiles, cache_page), take(len(noted_layers(reach, tiles, cache_page)))))
    pages = dict(zip(page_list(reach, tiles, cache_page), take(len(page_list(reach, tiles, cache_page)))))
    pages.update({(layer, 0): buffer for layer, buffer in noted.items()})
    ids_ref, top_ref, total_ref = (None,) * 3 if first else take(3)
    if first:
        ids_ref = take(1)[0]
    top_out, total_out = (None,) * 2 if last else take(2)
    outs = refs
    device = lax.axis_index("req")
    per_pack = lax.axis_size("req") // packs
    me = device % heads
    rows = 2 * PAGE
    width = heads * PAGE
    notes = {
        layer: buffer[2 * PAGE * heads :, :].astype(jnp.float32) for layer, buffer in noted.items()
    }

    def accumulate(used):
        keys, values, key_ids, key_places = [], [], [], []
        ones = jnp.ones((width, HD), jnp.bfloat16)
        lane = lax.broadcasted_iota(jnp.int32, (1, PAGE), 1)
        for layer, page in used:
            buffer = pages[layer, page]
            blocks = buffer.at[: 2 * PAGE * heads].reshape(heads, 2 * PAGE, HD)
            keys.append(blocks[:, :PAGE].reshape(width, HD))
            values.append(jnp.concatenate([blocks[:, PAGE:].reshape(width, HD), ones], axis=1))
            ids = [notes[layer][4 * bit + page : 4 * bit + page + 1] for bit in range(heads)]
            ids = jnp.concatenate(ids, axis=1)
            if layer > 0:
                same_pack = (device - layer * heads) // per_pack == device // per_pack
                ids = jnp.where(same_pack, ids, 0.0)
            key_ids.append(ids)
            key_places.append(
                jnp.concatenate(
                    [lane + ((me ^ bit) * rows + page * PAGE) for bit in range(heads)], axis=1
                )
            )
        wide = (PAGE, HD)
        for bit in range(heads):
            for page in range(2):
                at = pl.ds(page * PAGE, PAGE)
                query = queries[bit][at, :]
                if first:
                    query_ids = jnp.broadcast_to(
                        notes[0][4 * bit + page : 4 * bit + page + 1], wide
                    ).T
                    ids_ref[bit, at] = query_ids
                    place = lax.broadcasted_iota(jnp.int32, wide, 0) + ((me ^ bit) * rows + page * PAGE)
                    top = jnp.full(wide, MASKED, jnp.float32)
                    total = [jnp.zeros(wide, jnp.float32)] * 2
                else:
                    query_ids = ids_ref[bit, at]
                    top = top_ref[bit, at]
                    total = [total_ref[bit, at, half * HD : (half + 1) * HD] for half in range(2)]
                for index, (layer, _) in enumerate(used):
                    scores = lax.dot_general(
                        query, keys[index], (((1,), (1,)), ((), ())), preferred_element_type=jnp.float32
                    )
                    chunks = []
                    for other in range(heads):
                        lanes = slice(other * PAGE, (other + 1) * PAGE)
                        allowed = key_ids[index][:, lanes] == query_ids
                        if layer == 0:
                            allowed = allowed & (key_places[index][:, lanes] <= place)
                        chunks.append(jnp.where(allowed, scores[:, lanes], MASKED))
                    highest = jnp.max(functools.reduce(jnp.maximum, chunks), axis=1, keepdims=True)
                    higher = jnp.maximum(top, jnp.broadcast_to(highest, wide))
                    weights = jnp.concatenate(
                        [jnp.exp(chunk - higher).astype(jnp.bfloat16) for chunk in chunks], axis=1
                    )
                    shrink = jnp.exp(top - higher)
                    added = jnp.dot(weights, values[index], preferred_element_type=jnp.float32)
                    total = [total[half] * shrink + added[:, half * HD : (half + 1) * HD] for half in range(2)]
                    top = higher
                if last:
                    outs[bit][at, :] = (total[0] / total[1]).astype(jnp.bfloat16)
                else:
                    top_out[bit, at] = top
                    for half in range(2):
                        total_out[bit, at, half * HD : (half + 1) * HD] = total[half]

    if first:
        accumulate(tiles)
    else:
        (back,) = set(layer for layer, _ in tiles)
        present = (device - back * heads) // per_pack == device // per_pack
        pl.when(present)(lambda: accumulate(tiles))
        pl.when(jnp.logical_not(present))(lambda: accumulate([]))

    if cache_page is not None:
        select_pages(heads, reach, cache_page, device, notes, pages, outs, rows)


def select_pages(heads, reach, page, device, notes, pages, outs, start):
    me = device % heads
    sought = jnp.zeros((1, HD), jnp.int32)
    for bit in range(heads):
        for layer in range(reach + 1):
            for other in range(heads):
                if layer == 0 and other == bit:
                    continue
                distance = layer * heads + (me ^ bit) - (me ^ other)
                at = 4 * other + 2 + page
                hit = notes[layer][at : at + 1] == move(distance, page).astype(jnp.float32)
                place = (layer * heads + other + 1) << (6 * bit)
                sought = sought | jnp.where(hit & (distance > 0), place, 0)
    sought = jnp.max(sought)
    for bit in range(heads):
        found = ((sought >> (6 * bit)) & 63) - 1
        for layer in range(reach + 1):

            @pl.when((found >= layer * heads) & (found < (layer + 1) * heads))
            def _():
                at = pl.multiple_of((found - layer * heads) * (2 * PAGE), 2 * PAGE)
                outs[bit][start : start + 2 * PAGE, :] = pages[layer, page][pl.ds(at, 2 * PAGE), :]

        @pl.when(found < 0)
        def _():
            outs[bit][start : start + 2 * PAGE, :] = jnp.zeros((2 * PAGE, HD), jnp.bfloat16)


def select_kernel(heads, reach, *refs):
    buffers, outs = refs[: reach + 1], refs[reach + 1 :]
    notes = [buffer[2 * PAGE * heads :, :].astype(jnp.float32) for buffer in buffers]
    pages = {(layer, 0): buffer for layer, buffer in enumerate(buffers)}
    select_pages(heads, reach, 0, lax.axis_index("req"), notes, pages, outs, 0)


def noted_layers(reach, tiles, cache_page):
    layers = range(reach + 1) if cache_page is not None else [0] + [layer for layer, _ in tiles]
    return sorted(set(layers))


def page_list(reach, tiles, cache_page):
    wanted = list(tiles)
    if cache_page is not None:
        wanted += [(layer, cache_page) for layer in range(reach + 1)]
    return sorted(set(place for place in wanted if place[1] == 1))


def finish_kernel(heads, *refs):
    refs = list(refs)
    take = lambda count: [refs.pop(0) for _ in range(count)]
    final, early, own, (valid_ref,) = take(heads), take(heads), take(2 * heads), take(1)
    context_ref, cache_ref = refs
    device = lax.axis_index("req")
    me = device % heads
    rows = context_ref.shape[0]
    notes = own[0][2 * PAGE :, :].astype(jnp.float32)
    valid = valid_ref[...] > 0.0
    stays = [notes[2 + page : 3 + page] == move(0, page + 2) for page in range(2)]
    for bit in range(heads):
        lanes = pl.ds(pl.multiple_of((me ^ bit) * HD, HD), HD)
        context = final[bit][0:rows, :].astype(jnp.float32)
        context_ref[:, lanes] = jnp.where(valid, context, 0.0).astype(jnp.bfloat16)
        for part in range(2):
            first = part * PAGE
            cache_ref[0, part, :, lanes] = early[bit][first : first + PAGE, :]
            cache_ref[1, part, :, lanes] = final[bit][rows + first : rows + first + PAGE, :]
            for page in range(2):
                kept = own[2 * bit + page][first : first + PAGE, :].astype(jnp.float32)
                cache_ref[2 + page, part, :, lanes] = jnp.where(stays[page], kept, 0.0).astype(
                    jnp.bfloat16
                )


def per_device(tokens, norm_gain, norm_bias, w_qkv, segment_ids, pack_lengths, page_table):
    rows, features = tokens.shape
    tp = lax.axis_size("tp")
    local_width = w_qkv.shape[2]
    heads = local_width // HD
    reach = REACH // heads
    width = w_qkv.shape[0]
    packs = pack_lengths.shape[0]
    bf16 = jnp.bfloat16

    received = [paired(tokens, "tp", bit) for bit in range(1, tp)]
    weights = jnp.transpose(w_qkv, (1, 0, 2))
    lines = width // HD

    def placed(entries, row):
        below = NOTES + 2 * lines - row - entries.shape[0]
        return jnp.pad(entries, ((row, below), (0, HD - entries.shape[1])))

    ids, gain, bias = lax.optimization_barrier(
        (
            segment_ids.reshape(2, HD),
            norm_gain.reshape(lines, HD),
            norm_bias.reshape(lines, HD),
        )
    )
    integers = placed(ids, 0) + placed(page_table, 2)
    affine = placed(gain, NOTES) + placed(bias, NOTES + lines)
    table = integers.astype(jnp.float32) + affine.astype(jnp.float32)
    kept = pl.pallas_call(
        keep_kernel,
        out_shape=jax.ShapeDtypeStruct((rows, features), bf16),
        in_specs=[VMEM],
        out_specs=VMEM,
        compiler_params=pltpu.CompilerParams(vmem_limit_bytes=4 << 20),
        cost_estimate=cost(rows * features, 2 * rows * features),
        name="keep",
    )(tokens)

    piece_shapes = [(2 * PAGE + NOTES, HD), (2 * PAGE, HD)] * heads
    normed, valid, *own = pl.pallas_call(
        functools.partial(project_kernel, tp, heads),
        out_shape=[
            jax.ShapeDtypeStruct((rows, width), bf16),
            jax.ShapeDtypeStruct((rows, HD), jnp.float32),
        ]
        + [jax.ShapeDtypeStruct(shape, bf16) for shape in piece_shapes],
        in_specs=[SMEM, VMEM, HBM] + [VMEM] * tp,
        out_specs=[VMEM] * (2 + 2 * heads),
        scratch_shapes=[
            pltpu.VMEM((2, width, local_width), bf16),
            pltpu.VMEM((2, width), jnp.float32),
            pltpu.VMEM((rows, HD), jnp.float32),
            pltpu.VMEM((rows, local_width), bf16),
            pltpu.SemaphoreType.DMA((2,)),
        ],
        compiler_params=pltpu.CompilerParams(vmem_limit_bytes=PROJECT_VMEM),
        cost_estimate=cost(4 * rows * width * local_width, 4 * width * local_width),
        name="project",
    )(pack_lengths, kept, weights, table, *received)
    firsts, seconds = (
        [own[page]] + [paired(own[2 * bit + page], "req", bit) for bit in range(1, heads)]
        for page in range(2)
    )
    all_notes = sum(piece[2 * PAGE :] for piece in firsts)
    size = 2 * PAGE * heads + NOTES

    def laid(piece, row):
        return jnp.pad(piece, ((row, size - row - piece.shape[0]), (0, 0)))

    pages = [
        laid(all_notes, 2 * PAGE * heads)
        + sum(laid(piece[: 2 * PAGE], 2 * PAGE * bit) for bit, piece in enumerate(firsts)),
        jnp.stack(seconds).reshape(-1, HD),
    ]

    queries = pl.pallas_call(
        functools.partial(query_kernel, heads),
        out_shape=[jax.ShapeDtypeStruct((rows, HD), bf16)] * heads,
        in_specs=[VMEM, HBM],
        out_specs=[VMEM] * heads,
        scratch_shapes=[
            pltpu.VMEM((rows, local_width), bf16),
            pltpu.VMEM((width, local_width), bf16),
            pltpu.SemaphoreType.DMA,
        ],
        compiler_params=pltpu.CompilerParams(vmem_limit_bytes=24 << 20),
        cost_estimate=cost(2 * rows * width * local_width, 2 * width * local_width),
        name="queries",
    )(normed, weights)
    layers = [pages]
    queries = [queries[0]] + [paired(queries[bit], "req", bit) for bit in range(1, heads)]

    def ahead(buffer):
        return forward(buffer, "req", heads)

    layers.append([ahead(buffer) for buffer in layers[0]])

    state_shape = [
        jax.ShapeDtypeStruct((heads, rows, HD), jnp.float32),
        jax.ShapeDtypeStruct((heads, rows, 2 * HD), jnp.float32),
    ]

    def attend(tiles, state, last, cache_page):
        pairs = heads * rows * heads * PAGE * len(tiles)
        operands = (
            list(queries)
            + [layers[layer][0] for layer in noted_layers(reach, tiles, cache_page)]
            + [layers[layer][page] for layer, page in page_list(reach, tiles, cache_page)]
            + list(state)
        )
        if last:
            outs = [jax.ShapeDtypeStruct((rows + 2 * PAGE, HD), bf16)] * heads
        else:
            outs = ([] if state else state_shape[:1]) + state_shape + (
                [jax.ShapeDtypeStruct((2 * PAGE, HD), bf16)] * heads
                if cache_page is not None
                else []
            )
        return pl.pallas_call(
            functools.partial(
                attend_kernel, heads, reach, packs, tiles, not state, last, cache_page
            ),
            out_shape=outs,
            in_specs=[VMEM] * len(operands),
            out_specs=[VMEM] * len(outs),
            compiler_params=pltpu.CompilerParams(vmem_limit_bytes=32 << 20),
            cost_estimate=cost(6 * pairs * HD, 4 << 20, pairs),
            name="attend",
        )(*operands)

    ids, *state = attend([(0, 0), (0, 1)], [], False, None)
    first_page = layers[1][0]
    second_page, state = lax.optimization_barrier((layers[1][1], state))
    for _ in range(1, reach):
        first_page, second_page = ahead(first_page), ahead(second_page)
        layers.append([first_page, second_page])
    for layer in range(1, reach):
        state = attend([(layer, 0), (layer, 1)], [ids, *state], False, None)
    early = pl.pallas_call(
        functools.partial(select_kernel, heads, reach),
        out_shape=[jax.ShapeDtypeStruct((2 * PAGE, HD), bf16)] * heads,
        in_specs=[VMEM] * (reach + 1),
        out_specs=[VMEM] * heads,
        compiler_params=pltpu.CompilerParams(vmem_limit_bytes=8 << 20),
        cost_estimate=cost(0, 1 << 20),
        name="select",
    )(*[layer[0] for layer in layers])
    early = [early[0]] + [paired(early[bit], "req", bit) for bit in range(1, heads)]
    final = list(attend([(reach, 0), (reach, 1)], [ids, *state], True, 1))
    for bit in range(1, heads):
        final[bit], early[1 : bit + 1] = lax.optimization_barrier((final[bit], early[1 : bit + 1]))
    final = [final[0]] + [paired(final[bit], "req", bit) for bit in range(1, heads)]

    context, cache = pl.pallas_call(
        functools.partial(finish_kernel, heads),
        out_shape=[
            jax.ShapeDtypeStruct((rows, local_width), bf16),
            jax.ShapeDtypeStruct((4, 2, PAGE, local_width), bf16),
        ],
        in_specs=[VMEM] * (4 * heads + 1),
        out_specs=[VMEM] * 2,
        compiler_params=pltpu.CompilerParams(vmem_limit_bytes=16 << 20),
        name="finish",
    )(*final, *early, *own, valid)
    return context, cache


def solution(mesh):
    return jax.shard_map(
        per_device,
        mesh=mesh,
        in_specs=(P("req", "tp"), P(), P(), P(None, None, "tp"), P("req"), P(), P("req", None)),
        out_specs=(P("req", "tp"), P("req", None, None, "tp")),
        check_vma=False,
    )
```
